256 devices in a mesh: seq: 64 (over z_hi, y, x), chan: 4 (over z_lo, core).
Axes of the slice: x: 4, y: 4, z: 8 (z_hi: 4, z_lo: 2; z = z_hi * 2 + z_lo), core: 2. Of those that a mesh axis runs over, the one named last changes fastest.
Arguments:
- queries: bfloat16 [16384, 1024], P('seq', 'chan'), may hold values from -6 to 6
- keys: bfloat16 [16384, 1024], P('seq', 'chan'), may hold values from -6 to 6
- values: bfloat16 [16384, 1024], P('seq', 'chan'), may hold values from -6 to 6
- upstream: bfloat16 [16384, 1024], P('seq', 'chan'), may hold values from -6 to 6
- residues: float32 [1024, 16], P('chan'), may hold values from -1.5 to 1.5
- decay: float32 [1024, 16], P('chan'), may hold values from 3.0517578e-05 to 0.03
- skip: float32 [1024], P('chan'), may hold values from -3 to 3
Outputs:
- grad_queries: bfloat16 [16384, 1024], P('seq', 'chan')
- grad_keys: bfloat16 [16384, 1024], P('seq', 'chan')
- grad_values: bfloat16 [16384, 1024], P('seq', 'chan')
- grad_residues: float32 [1024, 16], P('chan')
- grad_decay: float32 [1024, 16], P('chan')
- grad_skip: float32 [1024], P('chan')
The draws below stay inside these ranges and needn't reach their ends.
All inputs are finite; a program needn't handle non-finite values.
Results may differ from the reference program's by a relative error of at most 0.013.
Values may be sent and summed in bfloat16 or wider, within the bound.
No kernel may reach another device: no remote copies, remote signals or barrier semaphores. Data moves between devices by JAX's collectives and lax.ppermute only.
A program may use at most 64 MiB of HBM per device.

```python
import math
import jax
import jax.numpy as jnp
from jax import lax

CHANNELS = 1024
MODES = 16
SEQLEN = 16384


def levels(rng, shape, pieces, least, high):
    gain, own = 1.0, jax.random.fold_in(rng, 6)
    for axis_at, parts in pieces:
        heights = jnp.exp(jax.random.uniform(jax.random.fold_in(own, axis_at), (parts,), jnp.float32, least / len(pieces), high / len(pieces)))
        gain = gain * jnp.repeat(heights, shape[axis_at] // parts).reshape([-1 if axis == axis_at else 1 for axis in range(len(shape))])
    return gain


def centred(key, shape, width, bound, pieces=(), kind=jnp.bfloat16):
    entries = width * jax.random.normal(key, shape, jnp.float32)
    if pieces:
        entries = entries * levels(key, shape, pieces, -0.22, 0.18)
    return jnp.clip(entries, -bound, bound).astype(kind)


def setup_inputs(seed: int = 0) -> dict:
    splits = jax.random.split(jax.random.key(seed), 8)
    return {
        "queries": centred(splits[0], (SEQLEN, CHANNELS), 1.0, 6.0, ((0, 64), (1, 4))),
        "keys": centred(splits[1], (SEQLEN, CHANNELS), 1.0, 6.0, ((0, 64), (1, 4))),
        "values": centred(splits[2], (SEQLEN, CHANNELS), 1.0, 6.0, ((0, 64), (1, 4))),
        "upstream": centred(splits[3], (SEQLEN, CHANNELS), 1.0, 6.0, ((0, 64), (1, 4))),
        "residues": centred(splits[4], (CHANNELS, MODES), 0.25, 1.5, ((0, 4),), jnp.float32),
        "decay": jnp.clip(jnp.exp(math.log(0.03) - 6.89065 * jax.random.uniform(splits[5], (CHANNELS, MODES), jnp.float32) ** levels(splits[5], (CHANNELS, MODES), ((0, 4),), -0.2, 0.2)), 3.0517578125e-05, 0.03),
        "skip": centred(splits[6], (CHANNELS,), 0.5, 3.0, ((0, 4),), jnp.float32),
    }


def reference(queries, keys, values, upstream, residues, decay, skip):
    length = queries.shape[0]
    total = 2 * length
    gated = (keys.astype(jnp.float32) * values.astype(jnp.float32)).astype(jnp.bfloat16)
    grad_conv = (upstream.astype(jnp.float32) * queries.astype(jnp.float32)).astype(jnp.bfloat16)
    gated_f = gated.astype(jnp.float32)
    grad_f = grad_conv.astype(jnp.float32)
    lags = jnp.arange(length, dtype=jnp.float32)
    roots = jnp.sqrt(decay)
    filt = jnp.zeros((length, queries.shape[1]), jnp.float32)
    for mode in range(decay.shape[1]):
        filt = filt + (residues[:, mode] * roots[:, mode])[None, :] * jnp.exp(-decay[:, mode][None, :] * lags[:, None])
    spec_filt = jnp.fft.rfft(filt, n=total, axis=0)
    spec_gated = jnp.fft.rfft(gated_f, n=total, axis=0)
    spec_grad = jnp.fft.rfft(grad_f, n=total, axis=0)
    conv_out = jnp.fft.irfft(spec_filt * spec_gated, n=total, axis=0)[:length] + skip[None, :] * gated_f
    conv_out = conv_out.astype(jnp.bfloat16)
    grad_queries = (upstream.astype(jnp.float32) * conv_out.astype(jnp.float32)).astype(jnp.bfloat16)
    grad_gated = jnp.fft.irfft(jnp.conj(spec_filt) * spec_grad, n=total, axis=0)[:length] + skip[None, :] * grad_f
    grad_gated = grad_gated.astype(jnp.bfloat16).astype(jnp.float32)
    grad_keys = (grad_gated * values.astype(jnp.float32)).astype(jnp.bfloat16)
    grad_values = (grad_gated * keys.astype(jnp.float32)).astype(jnp.bfloat16)
    grad_filt = jnp.fft.irfft(jnp.conj(spec_gated) * spec_grad, n=total, axis=0)[:length]
    res_list = []
    dec_list = []
    for mode in range(decay.shape[1]):
        expo = jnp.exp(-decay[:, mode][None, :] * lags[:, None])
        proj = lax.optimization_barrier(jnp.sum(grad_filt * expo, axis=0))
        tproj = lax.optimization_barrier(jnp.sum(grad_filt * lags[:, None] * expo, axis=0))
        res_list.append(roots[:, mode] * proj)
        dec_list.append(residues[:, mode] * (proj / (2.0 * roots[:, mode]) - roots[:, mode] * tproj))
    grad_residues = jnp.stack(res_list, axis=1)
    grad_decay = jnp.stack(dec_list, axis=1)
    grad_skip = lax.optimization_barrier(jnp.sum(grad_f * gated_f, axis=0))
    return (grad_queries, grad_keys, grad_values, grad_residues, grad_decay, grad_skip)
```

```python
import functools

import jax
import jax.numpy as jnp
from jax import lax
from jax.experimental import pallas as pl
from jax.experimental.pallas import tpu as pltpu
from jax.sharding import PartitionSpec as P

F32 = jnp.float32
BF16 = jnp.bfloat16
VMEM = pltpu.VMEM
SEGS = 8
LANES = 128
GROUP = 4


def product(a, b):
    return (a.astype(F32) * b.astype(F32)).astype(BF16).astype(F32)


def lanes_of(i):
    return pl.ds(pl.multiple_of(i * LANES, LANES), LANES)


def rows_of(i, n):
    return pl.ds(pl.multiple_of(i * n, n), n)


def fetch(sems, *pairs):
    copies = [pltpu.make_async_copy(a, b, sems.at[i]) for i, (a, b) in enumerate(pairs)]
    for copy in copies:
        copy.start()
    return copies


def summary_kernel(
    dec_hbm, k_hbm, v_hbm, u_hbm, q_hbm,
    z_ref, gated_ref, grad_ref, pre_ref, post_ref, dec_t_ref, k_ref, v_ref, u_ref, q_ref,
    w_ref, e_ref, e1_ref, g_ref, g1_ref, p_ref, t_ref, sems,
):
    copies = fetch(sems, (dec_hbm, dec_t_ref), (k_hbm, k_ref), (v_hbm, v_ref), (u_hbm, u_ref), (q_hbm, q_ref))
    rows, width = q_ref.shape
    modes = dec_t_ref.shape[0]
    steps = rows // SEGS
    tiles = width // LANES
    copies[0].wait()
    dec_t = dec_t_ref[...]
    w_all = jnp.exp(-dec_t)
    for i in range(tiles):
        for m in range(modes):
            row = w_all[m : m + 1, i * LANES : (i + 1) * LANES]
            w_ref[i, pl.ds(m * SEGS, SEGS), :] = jnp.broadcast_to(row, (SEGS, LANES))
    for copy in copies[1:]:
        copy.wait()
    skip = jnp.zeros((8, width), F32)
    for seg in range(SEGS):
        for part in range(steps // 16):
            at = pl.ds(seg * steps + part * 16, 16)
            gated = product(k_ref[at, :], v_ref[at, :])
            grad = product(u_ref[at, :], q_ref[at, :])
            both = gated * grad
            skip = skip + both[:8] + both[8:]
            to = pl.ds(part * 16 * SEGS + seg, 16, stride=SEGS)
            for i in range(tiles):
                ln = slice(i * LANES, (i + 1) * LANES)
                gated_ref[i, to, :] = gated[:, ln]
                grad_ref[i, to, :] = grad[:, ln]
    skip = jnp.sum(skip, axis=0, keepdims=True)

    groups = modes // GROUP

    def one(i, _):
        ln = lax.div(i, groups)
        base = lax.rem(i, groups) * GROUP
        at = [rows_of(base + m, SEGS) for m in range(GROUP)]
        w = [w_ref[ln, a, :] for a in at]
        zero = jnp.zeros((SEGS, LANES), F32)
        h, h1, p, t, r, r1 = ([zero] * GROUP for _ in range(6))
        for j in range(steps):
            x = gated_ref[ln, pl.ds(j * SEGS, SEGS), :]
            y = grad_ref[ln, pl.ds(j * SEGS, SEGS), :]
            back = grad_ref[ln, pl.ds((steps - 1 - j) * SEGS, SEGS), :]
            for m in range(GROUP):
                wh = w[m] * h[m]
                h1[m] = w[m] * h1[m] + wh
                h[m] = wh + x
                p[m] = p[m] + y * h[m]
                t[m] = t[m] + y * h1[m]
                wr = w[m] * r[m]
                r1[m] = w[m] * r1[m] + wr
                r[m] = wr + back
        for m in range(GROUP):
            e_ref[ln, at[m], :] = w[m] * h[m]
            e1_ref[ln, at[m], :] = w[m] * (h1[m] + h[m])
            g_ref[ln, at[m], :] = r[m]
            g1_ref[ln, at[m], :] = r1[m]
            p_ref[ln, at[m], :] = p[m]
            t_ref[ln, at[m], :] = t[m]
        return 0

    lax.fori_loop(0, groups * tiles, one, 0)

    for i in range(tiles):
        ln = slice(i * LANES, (i + 1) * LANES)
        dec = dec_t[:, ln]
        w_seg = jnp.exp(dec * (-float(steps)))
        zero = jnp.zeros((modes, LANES), F32)
        s, s1, p, t = zero, zero, zero, zero
        for seg in range(SEGS):
            at = pl.ds(seg, modes, stride=SEGS)
            g, g1 = g_ref[i, at, :], g1_ref[i, at, :]
            pre_ref[i, at, :] = s
            p = p + p_ref[i, at, :] + s * g
            t = t + t_ref[i, at, :] + s1 * g + s * g1
            s1 = w_seg * (s1 + float(steps) * s) + e1_ref[i, at, :]
            s = w_seg * s + e_ref[i, at, :]
        r, r1 = zero, zero
        for seg in range(SEGS - 1, -1, -1):
            at = pl.ds(seg, modes, stride=SEGS)
            post_ref[i, at, :] = r
            r1 = w_seg * (r1 + float(steps) * r) + g1_ref[i, at, :]
            r = w_seg * r + g_ref[i, at, :]
        parts = (s, 0.25 * s - dec * s1, r, 0.25 * r - dec * r1, p, 0.5 * p - dec * t)
        for n, part in enumerate(parts):
            z_ref[n * modes : (n + 1) * modes, ln] = part.astype(BF16)
    z_ref[6 * modes : 6 * modes + 16, :] = jnp.broadcast_to(skip, (16, width)).astype(BF16)


def conv_kernel(
    res_hbm, skip_hbm, gated_ref, grad_ref, dec_t_ref, pre_ref, post_ref,
    fwd_ref, bwd_ref, in_ref, out_ref, in0_ref, out0_ref, res_t_ref, skip_ref, w_ref, a_ref, sems,
):
    copies = fetch(sems, (res_hbm, res_t_ref), (skip_hbm, skip_ref))
    tiles, rows, _ = gated_ref.shape
    modes = dec_t_ref.shape[0]
    steps = rows // SEGS
    for copy in copies:
        copy.wait()
    dec_t = dec_t_ref[...]
    scale = res_t_ref[...] * jnp.sqrt(dec_t)
    seg_at = lax.broadcasted_iota(jnp.int32, (SEGS, LANES), 0).astype(F32) * float(steps)
    for i in range(tiles):
        ln = slice(i * LANES, (i + 1) * LANES)
        for m in range(modes):
            at = pl.ds(m * SEGS, SEGS)
            d = jnp.broadcast_to(dec_t[m : m + 1, ln], (SEGS, LANES))
            a = jnp.broadcast_to(scale[m : m + 1, ln], (SEGS, LANES))
            w = jnp.exp(-d)
            w_ref[i, at, :] = w
            a_ref[i, at, :] = a
            in_ref[i, at, :] = a * jnp.exp(-d * seg_at)
            out_ref[i, at, :] = a * jnp.exp(-d * (float(rows - steps + 1) - seg_at))
            in0_ref[i, at, :] = a * pre_ref[i, at, :]
            out0_ref[i, at, :] = a * w * post_ref[i, at, :]

    def one(i, _):
        for base in range(0, modes, GROUP):
            at = [pl.ds((base + m) * SEGS, SEGS) for m in range(GROUP)]
            w = [w_ref[i, x, :] for x in at]
            a = [a_ref[i, x, :] for x in at]
            zero = jnp.zeros((SEGS, LANES), F32)
            h, r = [zero] * GROUP, [zero] * GROUP
            for j in range(steps):
                at_f = pl.ds(j * SEGS, SEGS)
                at_b = pl.ds((steps - 1 - j) * SEGS, SEGS)
                x, y = gated_ref[i, at_f, :], grad_ref[i, at_b, :]
                f = fwd_ref[i, at_f, :] if base else zero
                b = bwd_ref[i, at_b, :] if base else zero
                for m in range(GROUP):
                    h[m] = w[m] * h[m] + x
                    r[m] = w[m] * r[m] + y
                    f = f + a[m] * h[m]
                    b = b + a[m] * r[m]
                fwd_ref[i, at_f, :] = f
                bwd_ref[i, at_b, :] = b
        return 0

    lax.fori_loop(0, tiles, one, 0)


def combine(level, count, own, got, dec_t, s, r):
    modes = dec_t.shape[0]
    at = lax.axis_index("seq")
    right = lax.rem(lax.div(at, 2**level), 2) == 1
    offset = lax.rem(at, 2**level).astype(F32)
    span = float(count * 2**level)

    def half(i, n=modes):
        mine = own[pl.ds(i * modes, n), :].astype(F32)
        other = got[pl.ds(i * modes, n), :].astype(F32)
        return jnp.where(right, other, mine), jnp.where(right, mine, other)

    e_l, e_r = half(0)
    f_l, f_r = half(1)
    g_l, g_r = half(2)
    h_l, h_r = half(3)
    p_l, p_r = half(4)
    d_l, d_r = half(5)
    k_l, k_r = half(6, 16)
    decay = jnp.exp(-dec_t * span)
    ds = dec_t * span
    block = (
        decay * e_l + e_r,
        decay * (f_l - ds * e_l) + f_r,
        g_l + decay * g_r,
        h_l + decay * (h_r - ds * g_r),
        p_l + p_r + e_l * g_r,
        d_l + d_r + f_l * g_r + e_l * h_r,
        k_l + k_r,
    )
    into = jnp.exp(dec_t * (-float(count) * offset)) * e_l
    back = jnp.exp(dec_t * (-float(count) * (float(2**level - 1) - offset))) * g_r
    return block, s + jnp.where(right, into, 0.0), r + jnp.where(right, 0.0, back)


def combine_kernel(level, count, own, got, dec_t_ref, s_ref, r_ref, z_ref, s_out, r_out):
    modes = dec_t_ref.shape[0]
    block, s, r = combine(level, count, own, got, dec_t_ref[...], s_ref[...], r_ref[...])
    for i, part in enumerate(block):
        z_ref[pl.ds(i * modes, part.shape[0]), :] = part.astype(BF16)
    s_out[...] = s
    r_out[...] = r


def finish_kernel(
    level, count,
    own, got, dec_t_ref, s_ref, r_ref, res_t_ref, skip_ref,
    q_ref, k_ref, v_ref, u_ref, fwd_ref, bwd_ref, in_ref, out_ref, in0_ref, out0_ref,
    dq_ref, dk_ref, dv_ref, dres_ref, ddec_ref, dskip_ref,
    f_ref, b_ref, sv_ref, rv_ref, w_ref,
):
    rows, width = q_ref.shape
    modes = dec_t_ref.shape[0]
    steps = rows // SEGS
    dec_t = dec_t_ref[...]
    block, s, r = combine(level, count, own, got, dec_t, s_ref[...], r_ref[...])
    roots = jnp.sqrt(dec_t)
    dres_ref[...] = roots * block[4]
    ddec_ref[...] = res_t_ref[...] / roots * block[5]
    dskip_ref[...] = block[6][:1]
    sv_ref[...] = s
    rv_ref[...] = r
    w_ref[...] = jnp.exp(-dec_t)

    def one(i, _):
        ln = lanes_of(i)

        def spread(ref, m):
            return jnp.broadcast_to(ref[pl.ds(m, 1), ln], (SEGS, LANES))

        w = [spread(w_ref, m) for m in range(modes)]
        at = [pl.ds(m * SEGS, SEGS) for m in range(modes)]
        c = [in_ref[i, at[m], :] * spread(sv_ref, m) + in0_ref[i, at[m], :] for m in range(modes)]
        for j in range(steps):
            here = pl.ds(j * SEGS, SEGS)
            f = fwd_ref[i, here, :]
            for m in range(modes):
                f = f + c[m]
                c[m] = c[m] * w[m]
            f_ref[i, here, :] = f
        c = [out_ref[i, at[m], :] * spread(rv_ref, m) + out0_ref[i, at[m], :] for m in range(modes)]
        for j in range(steps - 1, -1, -1):
            here = pl.ds(j * SEGS, SEGS)
            b = bwd_ref[i, here, :]
            for m in range(modes):
                b = b + c[m]
                c[m] = c[m] * w[m]
            b_ref[i, here, :] = b
        return 0

    lax.fori_loop(0, width // LANES, one, 0)

    for i in range(width // LANES):
        ln = slice(i * LANES, (i + 1) * LANES)
        skip = skip_ref[:, ln]
        for seg in range(SEGS):
            for part in range(steps // 16):
                at = slice(seg * steps + part * 16, seg * steps + part * 16 + 16)
                frm = pl.ds(part * 16 * SEGS + seg, 16, stride=SEGS)
                q, k, v, u = (ref[at, ln].astype(F32) for ref in (q_ref, k_ref, v_ref, u_ref))
                gated = (k * v).astype(BF16).astype(F32)
                grad = (u * q).astype(BF16).astype(F32)
                conv = (f_ref[i, frm, :] + skip * gated).astype(BF16).astype(F32)
                dq_ref[at, ln] = (u * conv).astype(BF16)
                gg = (b_ref[i, frm, :] + skip * grad).astype(BF16).astype(F32)
                dk_ref[at, ln] = (gg * v).astype(BF16)
                dv_ref[at, ln] = (gg * k).astype(BF16)


def kept(array, space=VMEM):
    return pltpu.with_memory_space_constraint(array, space)


def call(kernel, outs, args, scratch=(), flops=0, name=None, hbm=0):
    return pl.pallas_call(
        kernel,
        out_shape=outs,
        in_specs=[pl.BlockSpec(memory_space=pltpu.HBM)] * hbm + [pl.BlockSpec(memory_space=VMEM)] * (len(args) - hbm),
        out_specs=[pl.BlockSpec(memory_space=VMEM)] * len(outs),
        scratch_shapes=list(scratch),
        cost_estimate=pl.CostEstimate(flops=flops, bytes_accessed=1 << 19, transcendentals=0),
        compiler_params=pltpu.CompilerParams(vmem_limit_bytes=24 << 20),
        name=name,
    )(*[kept(a, pltpu.HBM) for a in args[:hbm]], *[kept(a) for a in args[hbm:]])


def exchange(array, mask, size):
    return lax.ppermute(array, "seq", [(i, i ^ mask) for i in range(size)])


def shards(queries, keys, values, upstream, residues, decay, skip):
    rows, width = queries.shape
    modes = residues.shape[1]
    size = lax.axis_size("seq")
    masks = (1, 3, 4, 12, 16, 48)
    seg_rows = modes * SEGS
    z_rows = 6 * modes + 16
    tiles = width // LANES
    big = VMEM((tiles, rows, LANES), F32)
    state = VMEM((modes, width), F32)
    spread = VMEM((tiles, seg_rows, LANES), F32)
    block = VMEM((z_rows, width), BF16)
    local = VMEM((rows, width), BF16)
    z, gated, grad, pre, post, dec_t, keys, values, upstream, queries = call(
        summary_kernel,
        [block, big, big, spread, spread, state] + [local] * 4,
        [decay.T, keys, values, upstream, queries],
        [spread] * 7 + [pltpu.SemaphoreType.DMA((5,))],
        flops=12 * rows * width * modes,
        name="summary",
        hbm=5,
    )
    fwd, bwd, in_w, out_w, in_0, out_0, res_t, skip = call(
        conv_kernel,
        [big, big, spread, spread, spread, spread, state, VMEM((1, width), F32)],
        [residues.T, skip.reshape(1, width), gated, grad, dec_t, pre, post],
        [spread] * 2 + [pltpu.SemaphoreType.DMA((2,))],
        flops=8 * rows * width * modes,
        name="conv",
        hbm=2,
    )
    s = jnp.zeros((modes, width), F32)
    r = jnp.zeros((modes, width), F32)
    for level, mask in enumerate(masks[:-1]):
        got = exchange(z, mask, size)
        z, s, r = call(
            functools.partial(combine_kernel, level, rows),
            [block, state, state],
            [z, got, dec_t, s, r],
            name=f"combine{level}",
        )
    got = exchange(z, masks[-1], size)
    outs = [jax.ShapeDtypeStruct((rows, width), BF16)] * 3
    outs += [jax.ShapeDtypeStruct((modes, width), F32)] * 2
    outs += [jax.ShapeDtypeStruct((1, width), F32)]
    dq, dk, dv, dres, ddec, dskip = call(
        functools.partial(finish_kernel, len(masks) - 1, rows),
        outs,
        [z, got, dec_t, s, r, res_t, skip, queries, keys, values, upstream, fwd, bwd, in_w, out_w, in_0, out_0],
        [big, big, state, state, state],
        name="finish",
    )
    return dq, dk, dv, dres.T, ddec.T, dskip.reshape(width)


def solution(mesh):
    tokens = P("seq", "chan")
    return jax.shard_map(
        shards,
        mesh=mesh,
        in_specs=(tokens, tokens, tokens, tokens, P("chan", None), P("chan", None), P("chan")),
        out_specs=(tokens, tokens, tokens, P("chan", None), P("chan", None), P("chan")),
        check_vma=False,
    )
```

```python
import functools

import jax
import jax.numpy as jnp
from jax import lax
from jax.experimental import pallas as pl
from jax.experimental.pallas import tpu as pltpu
from jax.sharding import PartitionSpec as P

F32 = jnp.float32
BF16 = jnp.bfloat16
VMEM = pltpu.VMEM
SEGS = 8
LANES = 128
GROUP = 4


def product(a, b):
    return (a.astype(F32) * b.astype(F32)).astype(BF16).astype(F32)


def lanes_of(i):
    return pl.ds(pl.multiple_of(i * LANES, LANES), LANES)


def rows_of(i, n):
    return pl.ds(pl.multiple_of(i * n, n), n)


def fetch(sems, *pairs):
    copies = [pltpu.make_async_copy(a, b, sems.at[i]) for i, (a, b) in enumerate(pairs)]
    for copy in copies:
        copy.start()
    return copies


def summary_kernel(
    dec_hbm, k_hbm, v_hbm, u_hbm, q_hbm,
    z_ref, gated_ref, grad_ref, pre_ref, post_ref, dec_t_ref, k_ref, v_ref, u_ref, q_ref,
    w_ref, e_ref, e1_ref, g_ref, g1_ref, p_ref, t_ref, sems,
):
    copies = fetch(sems, (dec_hbm, dec_t_ref), (k_hbm, k_ref), (v_hbm, v_ref), (u_hbm, u_ref), (q_hbm, q_ref))
    rows, width = q_ref.shape
    modes = dec_t_ref.shape[0]
    steps = rows // SEGS
    tiles = width // LANES
    copies[0].wait()
    dec_t = dec_t_ref[...]
    w_all = jnp.exp(-dec_t)
    for i in range(tiles):
        for m in range(modes):
            row = w_all[m : m + 1, i * LANES : (i + 1) * LANES]
            w_ref[i, pl.ds(m * SEGS, SEGS), :] = jnp.broadcast_to(row, (SEGS, LANES))
    for copy in copies[1:]:
        copy.wait()
    skip = jnp.zeros((8, width), F32)
    for seg in range(SEGS):
        for part in range(steps // 16):
            at = pl.ds(seg * steps + part * 16, 16)
            gated = product(k_ref[at, :], v_ref[at, :])
            grad = product(u_ref[at, :], q_ref[at, :])
            both = gated * grad
            skip = skip + both[:8] + both[8:]
            to = pl.ds(part * 16 * SEGS + seg, 16, stride=SEGS)
            for i in range(tiles):
                ln = slice(i * LANES, (i + 1) * LANES)
                gated_ref[i, to, :] = gated[:, ln]
                grad_ref[i, to, :] = grad[:, ln]
    skip = jnp.sum(skip, axis=0, keepdims=True)

    groups = modes // GROUP

    def one(i, _):
        ln = lax.div(i, groups)
        base = lax.rem(i, groups) * GROUP
        at = [rows_of(base + m, SEGS) for m in range(GROUP)]
        w = [w_ref[ln, a, :] for a in at]
        zero = jnp.zeros((SEGS, LANES), F32)
        h, h1, p, t, r, r1 = ([zero] * GROUP for _ in range(6))
        for j in range(steps):
            x = gated_ref[ln, pl.ds(j * SEGS, SEGS), :]
            y = grad_ref[ln, pl.ds(j * SEGS, SEGS), :]
            back = grad_ref[ln, pl.ds((steps - 1 - j) * SEGS, SEGS), :]
            for m in range(GROUP):
                wh = w[m] * h[m]
                h1[m] = w[m] * h1[m] + wh
                h[m] = wh + x
                p[m] = p[m] + y * h[m]
                t[m] = t[m] + y * h1[m]
                wr = w[m] * r[m]
                r1[m] = w[m] * r1[m] + wr
                r[m] = wr + back
        for m in range(GROUP):
            e_ref[ln, at[m], :] = w[m] * h[m]
            e1_ref[ln, at[m], :] = w[m] * (h1[m] + h[m])
            g_ref[ln, at[m], :] = r[m]
            g1_ref[ln, at[m], :] = r1[m]
            p_ref[ln, at[m], :] = p[m]
            t_ref[ln, at[m], :] = t[m]
        return 0

    lax.fori_loop(0, groups * tiles, one, 0)

    for i in range(tiles):
        ln = slice(i * LANES, (i + 1) * LANES)
        dec = dec_t[:, ln]
        w_seg = jnp.exp(dec * (-float(steps)))
        zero = jnp.zeros((modes, LANES), F32)
        s, s1, p, t = zero, zero, zero, zero
        for seg in range(SEGS):
            at = pl.ds(seg, modes, stride=SEGS)
            g, g1 = g_ref[i, at, :], g1_ref[i, at, :]
            pre_ref[i, at, :] = s
            p = p + p_ref[i, at, :] + s * g
            t = t + t_ref[i, at, :] + s1 * g + s * g1
            s1 = w_seg * (s1 + float(steps) * s) + e1_ref[i, at, :]
            s = w_seg * s + e_ref[i, at, :]
        r, r1 = zero, zero
        for seg in range(SEGS - 1, -1, -1):
            at = pl.ds(seg, modes, stride=SEGS)
            post_ref[i, at, :] = r
            r1 = w_seg * (r1 + float(steps) * r) + g1_ref[i, at, :]
            r = w_seg * r + g_ref[i, at, :]
        parts = (s, 0.25 * s - dec * s1, r, 0.25 * r - dec * r1, p, 0.5 * p - dec * t)
        for n, part in enumerate(parts):
            z_ref[n * modes : (n + 1) * modes, ln] = part.astype(BF16)
    z_ref[6 * modes : 6 * modes + 16, :] = jnp.broadcast_to(skip, (16, width)).astype(BF16)


def conv_kernel(
    res_hbm, skip_hbm, gated_ref, grad_ref, dec_t_ref, pre_ref, post_ref,
    fwd_ref, bwd_ref, in_ref, out_ref, in0_ref, out0_ref, res_t_ref, skip_ref, w_ref, a_ref, sems,
):
    copies = fetch(sems, (res_hbm, res_t_ref), (skip_hbm, skip_ref))
    tiles, rows, _ = gated_ref.shape
    modes = dec_t_ref.shape[0]
    steps = rows // SEGS
    for copy in copies:
        copy.wait()
    dec_t = dec_t_ref[...]
    scale = res_t_ref[...] * jnp.sqrt(dec_t)
    seg_at = lax.broadcasted_iota(jnp.int32, (SEGS, LANES), 0).astype(F32) * float(steps)
    for i in range(tiles):
        ln = slice(i * LANES, (i + 1) * LANES)
        for m in range(modes):
            at = pl.ds(m * SEGS, SEGS)
            d = jnp.broadcast_to(dec_t[m : m + 1, ln], (SEGS, LANES))
            a = jnp.broadcast_to(scale[m : m + 1, ln], (SEGS, LANES))
            w = jnp.exp(-d)
            w_ref[i, at, :] = w
            a_ref[i, at, :] = a
            in_ref[i, at, :] = a * jnp.exp(-d * seg_at)
            out_ref[i, at, :] = a * jnp.exp(-d * (float(rows - steps + 1) - seg_at))
            in0_ref[i, at, :] = a * pre_ref[i, at, :]
            out0_ref[i, at, :] = a * w * post_ref[i, at, :]

    def one(i, _):
        for base in range(0, modes, GROUP):
            at = [pl.ds((base + m) * SEGS, SEGS) for m in range(GROUP)]
            w = [w_ref[i, x, :] for x in at]
            a = [a_ref[i, x, :] for x in at]
            zero = jnp.zeros((SEGS, LANES), F32)
            h, r = [zero] * GROUP, [zero] * GROUP
            for j in range(steps):
                at_f = pl.ds(j * SEGS, SEGS)
                at_b = pl.ds((steps - 1 - j) * SEGS, SEGS)
                x, y = gated_ref[i, at_f, :], grad_ref[i, at_b, :]
                f = fwd_ref[i, at_f, :] if base else zero
                b = bwd_ref[i, at_b, :] if base else zero
                for m in range(GROUP):
                    h[m] = w[m] * h[m] + x
                    r[m] = w[m] * r[m] + y
                    f = f + a[m] * h[m]
                    b = b + a[m] * r[m]
                fwd_ref[i, at_f, :] = f
                bwd_ref[i, at_b, :] = b
        return 0

    lax.fori_loop(0, tiles, one, 0)


def combine(level, count, parts, dec_t, s, r):
    modes = dec_t.shape[0]
    at = lax.axis_index("seq")
    digit = lax.rem(lax.div(at, 4**level), 4)
    offset = lax.rem(at, 4**level).astype(F32)
    span = float(count * 4**level)

    def gather(i, n=modes):
        have = [part[pl.ds(i * modes, n), :].astype(F32) for part in parts]
        pick = []
        for j in range(4):
            away = digit ^ j
            pick.append(
                jnp.where(away >= 2, jnp.where(away == 2, have[2], have[3]), jnp.where(away == 0, have[0], have[1]))
            )
        return pick

    e, f, g, h, p, d = (gather(i) for i in range(6))
    k = gather(6, 16)
    one = dec_t * span
    w = [jnp.exp(one * (-float(j))) for j in range(4)]
    e_t, f_t, g_t, h_t, p_t, d_t, k_t = e[0], f[0], g[0], h[0], p[0], d[0], k[0]
    enter = jnp.zeros_like(s)
    for j in range(1, 4):
        enter = jnp.where(digit == j, e_t, enter)
        p_t = p_t + p[j] + e_t * g[j]
        d_t = d_t + d[j] + f_t * g[j] + e_t * h[j]
        f_t = w[1] * (f_t - one * e_t) + f[j]
        e_t = w[1] * e_t + e[j]
        h_t = h_t + w[j] * (h[j] - one * float(j) * g[j])
        g_t = g_t + w[j] * g[j]
        k_t = k_t + k[j]
    leave = jnp.zeros_like(r)
    tail = g[3]
    for j in range(2, -1, -1):
        leave = jnp.where(digit == j, tail, leave)
        tail = g[j] + w[1] * tail
    s = s + jnp.exp(dec_t * (-float(count) * offset)) * enter
    r = r + jnp.exp(dec_t * (-float(count) * (float(4**level - 1) - offset))) * leave
    return (e_t, f_t, g_t, h_t, p_t, d_t, k_t), s, r


def combine_kernel(level, count, z0, z1, z2, z3, dec_t_ref, s_ref, r_ref, z_ref, s_out, r_out):
    modes = dec_t_ref.shape[0]
    block, s, r = combine(level, count, (z0, z1, z2, z3), dec_t_ref[...], s_ref[...], r_ref[...])
    for i, part in enumerate(block):
        z_ref[pl.ds(i * modes, part.shape[0]), :] = part.astype(BF16)
    s_out[...] = s
    r_out[...] = r


def finish_kernel(
    level, count,
    z0, z1, z2, z3, dec_t_ref, s_ref, r_ref, res_t_ref, skip_ref,
    q_ref, k_ref, v_ref, u_ref, fwd_ref, bwd_ref, in_ref, out_ref, in0_ref, out0_ref,
    dq_ref, dk_ref, dv_ref, dres_ref, ddec_ref, dskip_ref,
    f_ref, b_ref, sv_ref, rv_ref, w_ref,
):
    rows, width = q_ref.shape
    modes = dec_t_ref.shape[0]
    steps = rows // SEGS
    dec_t = dec_t_ref[...]
    block, s, r = combine(level, count, (z0, z1, z2, z3), dec_t, s_ref[...], r_ref[...])
    roots = jnp.sqrt(dec_t)
    dres_ref[...] = roots * block[4]
    ddec_ref[...] = res_t_ref[...] / roots * block[5]
    dskip_ref[...] = block[6][:1]
    sv_ref[...] = s
    rv_ref[...] = r
    w_ref[...] = jnp.exp(-dec_t)

    def one(i, _):
        ln = lanes_of(i)

        def spread(ref, m):
            return jnp.broadcast_to(ref[pl.ds(m, 1), ln], (SEGS, LANES))

        w = [spread(w_ref, m) for m in range(modes)]
        at = [pl.ds(m * SEGS, SEGS) for m in range(modes)]
        c = [in_ref[i, at[m], :] * spread(sv_ref, m) + in0_ref[i, at[m], :] for m in range(modes)]
        for j in range(steps):
            here = pl.ds(j * SEGS, SEGS)
            f = fwd_ref[i, here, :]
            for m in range(modes):
                f = f + c[m]
                c[m] = c[m] * w[m]
            f_ref[i, here, :] = f
        c = [out_ref[i, at[m], :] * spread(rv_ref, m) + out0_ref[i, at[m], :] for m in range(modes)]
        for j in range(steps - 1, -1, -1):
            here = pl.ds(j * SEGS, SEGS)
            b = bwd_ref[i, here, :]
            for m in range(modes):
                b = b + c[m]
                c[m] = c[m] * w[m]
            b_ref[i, here, :] = b
        return 0

    lax.fori_loop(0, width // LANES, one, 0)

    for i in range(width // LANES):
        ln = slice(i * LANES, (i + 1) * LANES)
        skip = skip_ref[:, ln]
        for seg in range(SEGS):
            for part in range(steps // 16):
                at = slice(seg * steps + part * 16, seg * steps + part * 16 + 16)
                frm = pl.ds(part * 16 * SEGS + seg, 16, stride=SEGS)
                q, k, v, u = (ref[at, ln].astype(F32) for ref in (q_ref, k_ref, v_ref, u_ref))
                gated = (k * v).astype(BF16).astype(F32)
                grad = (u * q).astype(BF16).astype(F32)
                conv = (f_ref[i, frm, :] + skip * gated).astype(BF16).astype(F32)
                dq_ref[at, ln] = (u * conv).astype(BF16)
                gg = (b_ref[i, frm, :] + skip * grad).astype(BF16).astype(F32)
                dk_ref[at, ln] = (gg * v).astype(BF16)
                dv_ref[at, ln] = (gg * k).astype(BF16)


def kept(array, space=VMEM):
    return pltpu.with_memory_space_constraint(array, space)


def call(kernel, outs, args, scratch=(), flops=0, name=None, hbm=0):
    return pl.pallas_call(
        kernel,
        out_shape=outs,
        in_specs=[pl.BlockSpec(memory_space=pltpu.HBM)] * hbm + [pl.BlockSpec(memory_space=VMEM)] * (len(args) - hbm),
        out_specs=[pl.BlockSpec(memory_space=VMEM)] * len(outs),
        scratch_shapes=list(scratch),
        cost_estimate=pl.CostEstimate(flops=flops, bytes_accessed=1 << 19, transcendentals=0),
        compiler_params=pltpu.CompilerParams(vmem_limit_bytes=24 << 20),
        name=name,
    )(*[kept(a, pltpu.HBM) for a in args[:hbm]], *[kept(a) for a in args[hbm:]])


def exchange(array, level, size):
    got = {}
    for k in (2, 3, 1):
        got[k] = lax.ppermute(array, "seq", [(i, i ^ (k * 4**level)) for i in range(size)])
    return [array, got[1], got[2], got[3]]


def shards(queries, keys, values, upstream, residues, decay, skip):
    rows, width = queries.shape
    modes = residues.shape[1]
    size = lax.axis_size("seq")
    levels = 3
    seg_rows = modes * SEGS
    z_rows = 6 * modes + 16
    tiles = width // LANES
    big = VMEM((tiles, rows, LANES), F32)
    state = VMEM((modes, width), F32)
    spread = VMEM((tiles, seg_rows, LANES), F32)
    block = VMEM((z_rows, width), BF16)
    local = VMEM((rows, width), BF16)
    z, gated, grad, pre, post, dec_t, keys, values, upstream, queries = call(
        summary_kernel,
        [block, big, big, spread, spread, state] + [local] * 4,
        [decay.T, keys, values, upstream, queries],
        [spread] * 7 + [pltpu.SemaphoreType.DMA((5,))],
        flops=12 * rows * width * modes,
        name="summary",
        hbm=5,
    )
    fwd, bwd, in_w, out_w, in_0, out_0, res_t, skip = call(
        conv_kernel,
        [big, big, spread, spread, spread, spread, state, VMEM((1, width), F32)],
        [residues.T, skip.reshape(1, width), gated, grad, dec_t, pre, post],
        [spread] * 2 + [pltpu.SemaphoreType.DMA((2,))],
        flops=8 * rows * width * modes,
        name="conv",
        hbm=2,
    )
    s = jnp.zeros((modes, width), F32)
    r = jnp.zeros((modes, width), F32)
    for level in range(levels - 1):
        z, s, r = call(
            functools.partial(combine_kernel, level, rows),
            [block, state, state],
            [*exchange(z, level, size), dec_t, s, r],
            name=f"combine{level}",
        )
    outs = [jax.ShapeDtypeStruct((rows, width), BF16)] * 3
    outs += [jax.ShapeDtypeStruct((modes, width), F32)] * 2
    outs += [jax.ShapeDtypeStruct((1, width), F32)]
    dq, dk, dv, dres, ddec, dskip = call(
        functools.partial(finish_kernel, levels - 1, rows),
        outs,
        [*exchange(z, levels - 1, size), dec_t, s, r, res_t, skip, queries, keys, values, upstream, fwd, bwd, in_w, out_w, in_0, out_0],
        [big, big, state, state, state],
        name="finish",
    )
    return dq, dk, dv, dres.T, ddec.T, dskip.reshape(width)


def solution(mesh):
    tokens = P("seq", "chan")
    return jax.shard_map(
        shards,
        mesh=mesh,
        in_specs=(tokens, tokens, tokens, tokens, P("chan", None), P("chan", None), P("chan")),
        out_specs=(tokens, tokens, tokens, P("chan", None), P("chan", None), P("chan")),
        check_vma=False,
    )
```

```python
import functools

import jax
import jax.numpy as jnp
from jax import lax
from jax.experimental import pallas as pl
from jax.experimental.pallas import tpu as pltpu
from jax.sharding import PartitionSpec as P

F32 = jnp.float32
BF16 = jnp.bfloat16
VMEM = pltpu.VMEM
SEGS = 8
LANES = 128
GROUP = 4
HALF = 8


def product(a, b):
    return (a.astype(F32) * b.astype(F32)).astype(BF16).astype(F32)


def lanes_of(i):
    return pl.ds(pl.multiple_of(i * LANES, LANES), LANES)


def rows_of(i, n):
    return pl.ds(pl.multiple_of(i * n, n), n)


def fetch(sems, *pairs, first=0):
    copies = [pltpu.make_async_copy(a, b, sems.at[first + i]) for i, (a, b) in enumerate(pairs)]
    for copy in copies:
        copy.start()
    return copies


def summary_kernel(
    dec_hbm, k_hbm, v_hbm, u_hbm, q_hbm,
    z_ref, gated_ref, grad_ref, pre_ref, post_ref, dec_t_ref, k_ref, v_ref, u_ref, q_ref,
    w_ref, e_ref, e1_ref, g_ref, g1_ref, p_ref, t_ref, sems,
):
    rows, width = q_ref.shape
    modes = dec_t_ref.shape[0]
    steps = rows // SEGS
    tiles = width // LANES
    columns = [pl.ds(i * LANES, LANES) for i in range(tiles)]
    pairs = [(dec_hbm, dec_t_ref)]
    for ln in columns:
        pairs += [(a.at[:, ln], b.at[:, ln]) for a, b in ((k_hbm, k_ref), (v_hbm, v_ref), (u_hbm, u_ref), (q_hbm, q_ref))]
    copies = fetch(sems, *pairs)
    copies[0].wait()
    dec_t = dec_t_ref[...]
    w_all = jnp.exp(-dec_t)
    for i in range(tiles):
        for m in range(modes):
            row = w_all[m : m + 1, i * LANES : (i + 1) * LANES]
            w_ref[i, pl.ds(m * SEGS, SEGS), :] = jnp.broadcast_to(row, (SEGS, LANES))

    def one(base, i):
        at = [pl.ds((base * GROUP + m) * SEGS, SEGS) for m in range(GROUP)]
        w = [w_ref[i, a, :] for a in at]
        zero = jnp.zeros((SEGS, LANES), F32)
        h, h1, p, t, r, r1 = ([zero] * GROUP for _ in range(6))
        for j in range(steps):
            x = gated_ref[i, pl.ds(j * SEGS, SEGS), :]
            y = grad_ref[i, pl.ds(j * SEGS, SEGS), :]
            back = grad_ref[i, pl.ds((steps - 1 - j) * SEGS, SEGS), :]
            for m in range(GROUP):
                h[m] = w[m] * h[m] + x
                h1[m] = w[m] * h1[m] + h[m]
                p[m] = p[m] + y * h[m]
                t[m] = t[m] + y * h1[m]
                r[m] = w[m] * r[m] + back
                r1[m] = w[m] * r1[m] + r[m]
        for m in range(GROUP):
            e_ref[i, at[m], :] = w[m] * h[m]
            e1_ref[i, at[m], :] = w[m] * h1[m]
            g_ref[i, at[m], :] = r[m]
            g1_ref[i, at[m], :] = r1[m] - r[m]
            p_ref[i, at[m], :] = p[m]
            t_ref[i, at[m], :] = t[m] - p[m]

    for i, ln in enumerate(columns):
        for copy in copies[1 + 4 * i : 5 + 4 * i]:
            copy.wait()
        skip = jnp.zeros((8, LANES), F32)
        for seg in range(SEGS):
            for part in range(steps // 16):
                at = pl.ds(seg * steps + part * 16, 16)
                gated = product(k_ref[at, ln], v_ref[at, ln])
                grad = product(u_ref[at, ln], q_ref[at, ln])
                both = gated * grad
                skip = skip + both[:8] + both[8:]
                to = pl.ds(part * 16 * SEGS + seg, 16, stride=SEGS)
                gated_ref[i, to, :] = gated
                grad_ref[i, to, :] = grad
        skip = jnp.sum(skip, axis=0, keepdims=True)
        z_ref[6 * modes :, ln] = jnp.broadcast_to(skip, (8, LANES)).astype(BF16)
        for base in range(modes // GROUP):
            one(base, i)

    for i in range(tiles):
        ln = slice(i * LANES, (i + 1) * LANES)
        dec = dec_t[:, ln]
        w_seg = jnp.exp(dec * (-float(steps)))
        zero = jnp.zeros((modes, LANES), F32)
        s, s1, p, t = zero, zero, zero, zero
        for seg in range(SEGS):
            at = pl.ds(seg, modes, stride=SEGS)
            g, g1 = g_ref[i, at, :], g1_ref[i, at, :]
            pre_ref[i, at, :] = s
            p = p + p_ref[i, at, :] + s * g
            t = t + t_ref[i, at, :] + s1 * g + s * g1
            s1 = w_seg * (s1 + float(steps) * s) + e1_ref[i, at, :]
            s = w_seg * s + e_ref[i, at, :]
        r, r1 = zero, zero
        for seg in range(SEGS - 1, -1, -1):
            at = pl.ds(seg, modes, stride=SEGS)
            post_ref[i, at, :] = r
            r1 = w_seg * (r1 + float(steps) * r) + g1_ref[i, at, :]
            r = w_seg * r + g_ref[i, at, :]
        parts = (s, 0.25 * s - dec * s1, r, 0.25 * r - dec * r1, p, 0.5 * p - dec * t)
        for n, part in enumerate(parts):
            z_ref[n * modes : (n + 1) * modes, ln] = part.astype(BF16)


def conv_kernel(
    res_hbm, skip_hbm, gated_ref, grad_ref, dec_t_ref, pre_ref, post_ref,
    fwd_ref, bwd_ref, in_ref, out_ref, in0_ref, out0_ref, res_t_ref, skip_ref, w_ref, a_ref, sems,
):
    copies = fetch(sems, (res_hbm, res_t_ref), (skip_hbm, skip_ref))
    tiles, rows, _ = gated_ref.shape
    modes = dec_t_ref.shape[0]
    steps = rows // SEGS
    for copy in copies:
        copy.wait()
    dec_t = dec_t_ref[...]
    scale = res_t_ref[...] * jnp.sqrt(dec_t)
    seg_at = lax.broadcasted_iota(jnp.int32, (SEGS, LANES), 0).astype(F32) * float(steps)
    for i in range(tiles):
        ln = slice(i * LANES, (i + 1) * LANES)
        for m in range(modes):
            at = pl.ds(m * SEGS, SEGS)
            d = jnp.broadcast_to(dec_t[m : m + 1, ln], (SEGS, LANES))
            a = jnp.broadcast_to(scale[m : m + 1, ln], (SEGS, LANES))
            w = jnp.exp(-d)
            w_ref[i, at, :] = w
            a_ref[i, at, :] = a
            in_ref[i, at, :] = a * jnp.exp(-d * seg_at)
            out_ref[i, at, :] = a * jnp.exp(-d * (float(rows - steps + 1) - seg_at))
            in0_ref[i, at, :] = a * pre_ref[i, at, :]
            out0_ref[i, at, :] = a * w * post_ref[i, at, :]

    def one(i, _):
        direct = jnp.broadcast_to(skip_ref[:, lanes_of(i)], (SEGS, LANES))
        for base in range(0, modes, GROUP):
            at = [pl.ds((base + m) * SEGS, SEGS) for m in range(GROUP)]
            w = [w_ref[i, x, :] for x in at]
            a = [a_ref[i, x, :] for x in at]
            zero = jnp.zeros((SEGS, LANES), F32)
            h, r = [zero] * GROUP, [zero] * GROUP
            for j in range(steps):
                at_f = pl.ds(j * SEGS, SEGS)
                at_b = pl.ds((steps - 1 - j) * SEGS, SEGS)
                x, y = gated_ref[i, at_f, :], grad_ref[i, at_b, :]
                f = fwd_ref[i, at_f, :] if base else direct * x
                b = bwd_ref[i, at_b, :] if base else direct * y
                for m in range(GROUP):
                    h[m] = w[m] * h[m] + x
                    r[m] = w[m] * r[m] + y
                    f = f + a[m] * h[m]
                    b = b + a[m] * r[m]
                fwd_ref[i, at_f, :] = f
                bwd_ref[i, at_b, :] = b
        return 0

    lax.fori_loop(0, tiles, one, 0)


def combine(level, count, parts, dec_t, s, r):
    modes = dec_t.shape[0]
    at = lax.axis_index("seq")
    digit = lax.rem(lax.div(at, 4**level), 4)
    offset = lax.rem(at, 4**level).astype(F32)
    span = float(count * 4**level)

    def gather(i, n=modes):
        have = [part[pl.ds(i * modes, n), :].astype(F32) for part in parts]
        pick = []
        for j in range(4):
            away = digit ^ j
            pick.append(
                jnp.where(away >= 2, jnp.where(away == 2, have[2], have[3]), jnp.where(away == 0, have[0], have[1]))
            )
        return pick

    e, f, g, h, p, d = (gather(i) for i in range(6))
    k = gather(6, 8)
    one = dec_t * span
    w = [jnp.exp(one * (-float(j))) for j in range(4)]
    e_t, f_t, g_t, h_t, p_t, d_t, k_t = e[0], f[0], g[0], h[0], p[0], d[0], k[0]
    enter = jnp.zeros_like(s)
    for j in range(1, 4):
        enter = jnp.where(digit == j, e_t, enter)
        p_t = p_t + p[j] + e_t * g[j]
        d_t = d_t + d[j] + f_t * g[j] + e_t * h[j]
        f_t = w[1] * (f_t - one * e_t) + f[j]
        e_t = w[1] * e_t + e[j]
        h_t = h_t + w[j] * (h[j] - one * float(j) * g[j])
        g_t = g_t + w[j] * g[j]
        k_t = k_t + k[j]
    leave = jnp.zeros_like(r)
    tail = g[3]
    for j in range(2, -1, -1):
        leave = jnp.where(digit == j, tail, leave)
        tail = g[j] + w[1] * tail
    s = s + jnp.exp(dec_t * (-float(count) * offset)) * enter
    r = r + jnp.exp(dec_t * (-float(count) * (float(4**level - 1) - offset))) * leave
    return (e_t, f_t, g_t, h_t, p_t, d_t, k_t), s, r


def combine_kernel(level, count, z0, z1, z3, z2, dec_t_ref, s_ref, r_ref, z_ref, s_out, r_out):
    modes = dec_t_ref.shape[0]
    block, s, r = combine(level, count, (z0, z1, z2, z3), dec_t_ref[...], s_ref[...], r_ref[...])
    for i, part in enumerate(block):
        z_ref[pl.ds(i * modes, part.shape[0]), :] = part.astype(BF16)
    s_out[...] = s
    r_out[...] = r


def finish_kernel(
    level, count,
    z0, z1, z3, z2, dec_t_ref, s_ref, r_ref, res_t_ref,
    k_ref, v_ref, u_ref, fwd_ref, bwd_ref, in_ref, out_ref, in0_ref, out0_ref,
    dq_hbm, dk_hbm, dv_hbm, dres_hbm, ddec_hbm, dskip_hbm,
    dq_ref, dk_ref, dv_ref, dres_ref, ddec_ref, dskip_ref, f_ref, b_ref, sv_ref, rv_ref, w_ref, sems,
):
    rows, width = k_ref.shape
    modes = dec_t_ref.shape[0]
    steps = rows // SEGS
    dec_t = dec_t_ref[...]
    block, s, r = combine(level, count, (z0, z1, z2, z3), dec_t, s_ref[...], r_ref[...])
    sv_ref[...] = s
    rv_ref[...] = r
    w_ref[...] = jnp.exp(-dec_t)
    roots = jnp.sqrt(dec_t)
    dres_ref[...] = roots * block[4]
    ddec_ref[...] = res_t_ref[...] / roots * block[5]
    dskip_ref[...] = block[6][:1]
    copies = fetch(sems, (dres_ref, dres_hbm), (ddec_ref, ddec_hbm), (dskip_ref, dskip_hbm))

    def one(i, _):
        ln = lanes_of(i)

        def spread(ref, m):
            return jnp.broadcast_to(ref[pl.ds(m, 1), ln], (SEGS, LANES))

        for half in range(0, modes, HALF):
            w = [spread(w_ref, half + m) for m in range(HALF)]
            powers = [[x, x * x, x * x * x, (x * x) * (x * x)] for x in w]
            at = [pl.ds((half + m) * SEGS, SEGS) for m in range(HALF)]
            sides = (
                (in_ref, in0_ref, sv_ref, fwd_ref, f_ref, range(steps)),
                (out_ref, out0_ref, rv_ref, bwd_ref, b_ref, range(steps - 1, -1, -1)),
            )
            for scale, extra, state, local, total, order in sides:
                c = [scale[i, at[m], :] * spread(state, half + m) + extra[i, at[m], :] for m in range(HALF)]
                source = total if half else local
                for first in range(0, steps, 4):
                    here = [pl.ds(j * SEGS, SEGS) for j in order[first : first + 4]]
                    y = [source[i, x, :] for x in here]
                    for m in range(HALF):
                        w1, w2, w3, w4 = powers[m]
                        y[0] = y[0] + c[m]
                        y[1] = y[1] + c[m] * w1
                        y[2] = y[2] + c[m] * w2
                        y[3] = y[3] + c[m] * w3
                        if first < steps - 4:
                            c[m] = c[m] * w4
                    for x, value in zip(here, y):
                        total[i, x, :] = value
        return 0

    lax.fori_loop(0, width // LANES, one, 0)

    done = 0
    for seg in range(SEGS):
        for part in range(steps // 16):
            to = pl.ds(seg * steps + part * 16, 16)
            frm = pl.ds(part * 16 * SEGS + seg, 16, stride=SEGS)
            for i in range(width // LANES):
                ln = pl.ds(i * LANES, LANES)
                conv = f_ref[i, frm, :].astype(BF16).astype(F32)
                gg = b_ref[i, frm, :].astype(BF16).astype(F32)
                dq_ref[to, ln] = (u_ref[to, ln].astype(F32) * conv).astype(BF16)
                dk_ref[to, ln] = (gg * v_ref[to, ln].astype(F32)).astype(BF16)
                dv_ref[to, ln] = (gg * k_ref[to, ln].astype(F32)).astype(BF16)
        if seg % 2:
            block_rows = pl.ds((seg - 1) * steps, 2 * steps)
            pairs = ((dq_ref, dq_hbm), (dk_ref, dk_hbm), (dv_ref, dv_hbm))
            copies += fetch(sems, *[(a.at[block_rows], b.at[block_rows]) for a, b in pairs], first=3 + 3 * (seg // 2))
    for copy in copies:
        copy.wait()


def kept(array, space=VMEM):
    return pltpu.with_memory_space_constraint(array, space)


def call(kernel, outs, args, scratch=(), flops=0, name=None, hbm=0, out_space=VMEM):
    return pl.pallas_call(
        kernel,
        out_shape=outs,
        in_specs=[pl.BlockSpec(memory_space=pltpu.HBM)] * hbm + [pl.BlockSpec(memory_space=VMEM)] * (len(args) - hbm),
        out_specs=[pl.BlockSpec(memory_space=out_space)] * len(outs),
        scratch_shapes=list(scratch),
        cost_estimate=pl.CostEstimate(flops=flops, bytes_accessed=1 << 19, transcendentals=0),
        compiler_params=pltpu.CompilerParams(vmem_limit_bytes=24 << 20),
        name=name,
    )(*[kept(a, pltpu.HBM) for a in args[:hbm]], *[kept(a) for a in args[hbm:]])


def exchange(array, level, size):
    got = {}
    for k in (1, 3, 2):
        got[k] = lax.ppermute(array, "seq", [(i, i ^ (k * 4**level)) for i in range(size)])
    return [array, got[1], got[3], got[2]]


def shards(queries, keys, values, upstream, residues, decay, skip):
    rows, width = queries.shape
    modes = residues.shape[1]
    size = lax.axis_size("seq")
    levels = 3
    seg_rows = modes * SEGS
    z_rows = 6 * modes + 8
    tiles = width // LANES
    big = VMEM((tiles, rows, LANES), F32)
    state = VMEM((modes, width), F32)
    spread = VMEM((tiles, seg_rows, LANES), F32)
    block = VMEM((z_rows, width), BF16)
    local = VMEM((rows, width), BF16)
    z, gated, grad, pre, post, dec_t, keys, values, upstream, queries = call(
        summary_kernel,
        [block, big, big, spread, spread, state] + [local] * 4,
        [decay.T, keys, values, upstream, queries],
        [spread] * 7 + [pltpu.SemaphoreType.DMA((1 + 4 * tiles,))],
        flops=12 * rows * width * modes,
        name="summary",
        hbm=5,
    )
    fwd, bwd, in_w, out_w, in_0, out_0, res_t, skip = call(
        conv_kernel,
        [big, big, spread, spread, spread, spread, state, VMEM((1, width), F32)],
        [residues.T, skip.reshape(1, width), gated, grad, dec_t, pre, post],
        [spread] * 2 + [pltpu.SemaphoreType.DMA((2,))],
        flops=8 * rows * width * modes,
        name="conv",
        hbm=2,
    )
    s = jnp.zeros((modes, width), F32)
    r = jnp.zeros((modes, width), F32)
    for level in range(levels - 1):
        z, s, r = call(
            functools.partial(combine_kernel, level, rows),
            [block, state, state],
            [*exchange(z, level, size), dec_t, s, r],
            name=f"combine{level}",
        )
    outs = [jax.ShapeDtypeStruct((rows, width), BF16)] * 3
    outs += [jax.ShapeDtypeStruct((modes, width), F32)] * 2
    outs += [jax.ShapeDtypeStruct((1, width), F32)]
    dq, dk, dv, dres, ddec, dskip = call(
        functools.partial(finish_kernel, levels - 1, rows),
        outs,
        [*exchange(z, levels - 1, size), dec_t, s, r, res_t, keys, values, upstream, fwd, bwd, in_w, out_w, in_0, out_0],
        [local] * 3 + [state] * 2 + [VMEM((1, width), F32), big, big, state, state, state, pltpu.SemaphoreType.DMA((3 + 3 * SEGS // 2,))],
        name="finish",
        out_space=pltpu.HBM,
    )
    return dq, dk, dv, dres.T, ddec.T, dskip.reshape(width)


def solution(mesh):
    tokens = P("seq", "chan")
    return jax.shard_map(
        shards,
        mesh=mesh,
        in_specs=(tokens, tokens, tokens, tokens, P("chan", None), P("chan", None), P("chan")),
        out_specs=(tokens, tokens, tokens, P("chan", None), P("chan", None), P("chan")),
        check_vma=False,
    )
```

```python
import functools

import jax
import jax.numpy as jnp
from jax import lax
from jax.experimental import pallas as pl
from jax.experimental.pallas import tpu as pltpu
from jax.sharding import PartitionSpec as P

F32 = jnp.float32
BF16 = jnp.bfloat16
VMEM = pltpu.VMEM
SEGS = 8
LANES = 128
GROUP = 4


def product(a, b):
    return (a.astype(F32) * b.astype(F32)).astype(BF16).astype(F32)


def lanes_of(i):
    return pl.ds(pl.multiple_of(i * LANES, LANES), LANES)


def rows_of(i, n):
    return pl.ds(pl.multiple_of(i * n, n), n)


def fetch(sems, *pairs, first=0):
    copies = [pltpu.make_async_copy(a, b, sems.at[first + i]) for i, (a, b) in enumerate(pairs)]
    for copy in copies:
        copy.start()
    return copies


def summary_kernel(
    dec_hbm, k_hbm, v_hbm, u_hbm, q_hbm,
    z_ref, gated_ref, grad_ref, pre_ref, post_ref, dec_t_ref, k_ref, v_ref, u_ref, q_ref,
    w_ref, e_ref, e1_ref, g_ref, g1_ref, p_ref, t_ref, sems,
):
    rows, width = q_ref.shape
    modes = dec_t_ref.shape[0]
    steps = rows // SEGS
    tiles = width // LANES
    columns = [pl.ds(i * LANES, LANES) for i in range(tiles)]
    pairs = [(dec_hbm, dec_t_ref)]
    for ln in columns:
        pairs += [(a.at[:, ln], b.at[:, ln]) for a, b in ((k_hbm, k_ref), (v_hbm, v_ref), (u_hbm, u_ref), (q_hbm, q_ref))]
    copies = fetch(sems, *pairs)
    copies[0].wait()
    dec_t = dec_t_ref[...]
    w_all = jnp.exp(-dec_t)
    for i in range(tiles):
        for m in range(modes):
            row = w_all[m : m + 1, i * LANES : (i + 1) * LANES]
            w_ref[i, pl.ds(m * SEGS, SEGS), :] = jnp.broadcast_to(row, (SEGS, LANES))

    def one(base, i):
        at = [pl.ds((base * GROUP + m) * SEGS, SEGS) for m in range(GROUP)]
        w = [w_ref[i, a, :] for a in at]
        zero = jnp.zeros((SEGS, LANES), F32)
        h, h1, p, t, r, r1 = ([zero] * GROUP for _ in range(6))
        for j in range(steps):
            x = gated_ref[i, pl.ds(j * SEGS, SEGS), :]
            y = grad_ref[i, pl.ds(j * SEGS, SEGS), :]
            back = grad_ref[i, pl.ds((steps - 1 - j) * SEGS, SEGS), :]
            for m in range(GROUP):
                h[m] = w[m] * h[m] + x
                h1[m] = w[m] * h1[m] + h[m]
                p[m] = p[m] + y * h[m]
                t[m] = t[m] + y * h1[m]
                r[m] = w[m] * r[m] + back
                r1[m] = w[m] * r1[m] + r[m]
        for m in range(GROUP):
            e_ref[i, at[m], :] = w[m] * h[m]
            e1_ref[i, at[m], :] = w[m] * h1[m]
            g_ref[i, at[m], :] = r[m]
            g1_ref[i, at[m], :] = r1[m] - r[m]
            p_ref[i, at[m], :] = p[m]
            t_ref[i, at[m], :] = t[m] - p[m]

    for i, ln in enumerate(columns):
        for copy in copies[1 + 4 * i : 5 + 4 * i]:
            copy.wait()
        skip = jnp.zeros((8, LANES), F32)
        for seg in range(SEGS):
            for part in range(steps // 16):
                at = pl.ds(seg * steps + part * 16, 16)
                gated = product(k_ref[at, ln], v_ref[at, ln])
                grad = product(u_ref[at, ln], q_ref[at, ln])
                both = gated * grad
                skip = skip + both[:8] + both[8:]
                to = pl.ds(part * 16 * SEGS + seg, 16, stride=SEGS)
                gated_ref[i, to, :] = gated
                grad_ref[i, to, :] = grad
        skip = jnp.sum(skip, axis=0, keepdims=True)
        z_ref[6 * modes :, ln] = jnp.broadcast_to(skip, (8, LANES)).astype(BF16)
        for base in range(modes // GROUP):
            one(base, i)

    for i in range(tiles):
        ln = slice(i * LANES, (i + 1) * LANES)
        dec = dec_t[:, ln]
        w_seg = jnp.exp(dec * (-float(steps)))
        zero = jnp.zeros((modes, LANES), F32)
        s, s1, p, t = zero, zero, zero, zero
        for seg in range(SEGS):
            at = pl.ds(seg, modes, stride=SEGS)
            g, g1 = g_ref[i, at, :], g1_ref[i, at, :]
            pre_ref[i, at, :] = s
            p = p + p_ref[i, at, :] + s * g
            t = t + t_ref[i, at, :] + s1 * g + s * g1
            s1 = w_seg * (s1 + float(steps) * s) + e1_ref[i, at, :]
            s = w_seg * s + e_ref[i, at, :]
        r, r1 = zero, zero
        for seg in range(SEGS - 1, -1, -1):
            at = pl.ds(seg, modes, stride=SEGS)
            post_ref[i, at, :] = r
            r1 = w_seg * (r1 + float(steps) * r) + g1_ref[i, at, :]
            r = w_seg * r + g_ref[i, at, :]
        parts = (s, 0.25 * s - dec * s1, r, 0.25 * r - dec * r1, p, 0.5 * p - dec * t)
        for n, part in enumerate(parts):
            z_ref[n * modes : (n + 1) * modes, ln] = part.astype(BF16)


def place(stride, radix):
    at = lax.axis_index("seq")
    return lax.rem(lax.div(at, stride), radix), lax.rem(at, stride)


def conv_kernel(
    stride, count,
    res_hbm, skip_hbm, gated_ref, grad_ref, dec_t_ref, pre_ref, post_ref, s_ref, r_ref, k_ref, v_ref, u_ref,
    fwd_ref, bwd_ref, scale_ref, roots_ref, ratio_ref, dq_ref, dk_ref, dv_ref,
    res_t_ref, skip_ref, w_ref, a_ref, h_ref, b_ref, sems,
):
    copies = fetch(sems, (res_hbm, res_t_ref), (skip_hbm, skip_ref))
    tiles, rows, _ = gated_ref.shape
    modes = dec_t_ref.shape[0]
    steps = rows // SEGS
    digit, offset = place(stride, 2)
    right = digit == 1
    chunks = jnp.where(right, offset, stride - 1 - offset).astype(F32)
    for copy in copies:
        copy.wait()
    dec_t = dec_t_ref[...]
    roots = jnp.sqrt(dec_t)
    scale = res_t_ref[...] * roots
    roots_ref[...] = roots
    ratio_ref[...] = res_t_ref[...] / roots
    far = scale * jnp.exp(dec_t * (-float(count) * chunks))
    s, r = s_ref[...], r_ref[...]
    seg_at = lax.broadcasted_iota(jnp.int32, (SEGS, LANES), 0).astype(F32) * float(steps)
    away = jnp.where(right, seg_at, float(rows - steps + 1) - seg_at)
    for i in range(tiles):
        ln = slice(i * LANES, (i + 1) * LANES)
        for m in range(modes):
            at = pl.ds(m * SEGS, SEGS)

            def spread(x):
                return jnp.broadcast_to(x[m : m + 1, ln], (SEGS, LANES))

            d = spread(dec_t)
            w_ref[i, at, :] = jnp.exp(-d)
            a_ref[i, at, :] = spread(scale)
            scale_ref[i, at, :] = spread(far) * jnp.exp(-d * away)
            h_ref[i, at, :] = pre_ref[i, at, :] + jnp.exp(-d * seg_at) * spread(s)
            b_ref[i, at, :] = post_ref[i, at, :] + jnp.exp(-d * (float(rows - steps) - seg_at)) * spread(r)

    def one(i, _):
        direct = jnp.broadcast_to(skip_ref[:, lanes_of(i)], (SEGS, LANES))
        for base in range(0, modes, GROUP):
            at = [pl.ds((base + m) * SEGS, SEGS) for m in range(GROUP)]
            w = [w_ref[i, x, :] for x in at]
            a = [a_ref[i, x, :] for x in at]
            h = [h_ref[i, x, :] for x in at]
            r = [b_ref[i, x, :] for x in at]
            for j in range(steps):
                at_f = pl.ds(j * SEGS, SEGS)
                at_b = pl.ds((steps - 1 - j) * SEGS, SEGS)
                x, y = gated_ref[i, at_f, :], grad_ref[i, at_b, :]
                f = fwd_ref[i, at_f, :] if base else direct * x
                b = bwd_ref[i, at_b, :] if base else direct * y
                for m in range(GROUP):
                    h[m] = (w[m] * h[m] if j else h[m]) + x
                    r[m] = w[m] * r[m] + y
                    f = f + a[m] * h[m]
                    b = b + a[m] * r[m]
                fwd_ref[i, at_f, :] = f
                bwd_ref[i, at_b, :] = b
        return 0

    lax.fori_loop(0, tiles, one, 0)
    for seg in range(SEGS):
        for part in range(steps // 16):
            to, frm = rows_in(seg, part, steps)
            for i in range(tiles):
                ln = pl.ds(i * LANES, LANES)
                query_rows(u_ref, fwd_ref, dq_ref, i, frm, to, ln)
                pair_rows(k_ref, v_ref, bwd_ref, dk_ref, dv_ref, i, frm, to, ln)


def rows_in(seg, part, steps):
    return pl.ds(seg * steps + part * 16, 16), pl.ds(part * 16 * SEGS + seg, 16, stride=SEGS)


def query_rows(u_ref, total_ref, dq_ref, i, frm, to, ln):
    conv = total_ref[i, frm, :].astype(BF16).astype(F32)
    dq_ref[to, ln] = (u_ref[to, ln].astype(F32) * conv).astype(BF16)


def pair_rows(k_ref, v_ref, total_ref, dk_ref, dv_ref, i, frm, to, ln):
    gg = total_ref[i, frm, :].astype(BF16).astype(F32)
    dk_ref[to, ln] = (gg * v_ref[to, ln].astype(F32)).astype(BF16)
    dv_ref[to, ln] = (gg * k_ref[to, ln].astype(F32)).astype(BF16)


def four_kernel(stride, count, z0, z1, z3, z2, *refs):
    combine_kernel(stride, 4, count, False, z0, z1, z2, z3, *refs)


def combine_kernel(stride, radix, count, last, *refs):
    parts = refs[:radix]
    dec_t_ref, s_ref, r_ref, z_ref, s_out, r_out = refs[radix : radix + 6]
    dec_t = dec_t_ref[...]
    modes = dec_t.shape[0]
    digit, offset = place(stride, radix)
    offset = offset.astype(F32)

    def gather(i, n=modes):
        have = [part[pl.ds(i * modes, n), :].astype(F32) for part in parts]
        pick = []
        for j in range(radix):
            k = digit ^ j
            first = jnp.where(k == 0, have[0], have[1])
            if radix == 4:
                first = jnp.where(k >= 2, jnp.where(k == 2, have[2], have[3]), first)
            pick.append(first)
        return pick

    e, f, g, h, p, d = (gather(i) for i in range(6))
    k = gather(6, 8)
    one = dec_t * float(count * stride)
    w = [jnp.exp(one * (-float(j))) for j in range(radix)]
    e_t, f_t, g_t, h_t, p_t, d_t, k_t = e[0], f[0], g[0], h[0], p[0], d[0], k[0]
    enter = jnp.zeros_like(dec_t)
    for j in range(1, radix):
        enter = jnp.where(digit == j, e_t, enter)
        p_t = p_t + p[j] + e_t * g[j]
        d_t = d_t + d[j] + f_t * g[j] + e_t * h[j]
        f_t = w[1] * (f_t - one * e_t) + f[j]
        e_t = w[1] * e_t + e[j]
        h_t = h_t + w[j] * (h[j] - one * float(j) * g[j])
        g_t = g_t + w[j] * g[j]
        k_t = k_t + k[j]
    leave = jnp.zeros_like(dec_t)
    tail = g[-1]
    for j in range(radix - 2, -1, -1):
        leave = jnp.where(digit == j, tail, leave)
        tail = g[j] + w[1] * tail
    s_out[...] = s_ref[...] + jnp.exp(dec_t * (-float(count) * offset)) * enter
    r_out[...] = r_ref[...] + jnp.exp(dec_t * (-float(count) * (float(stride - 1) - offset))) * leave
    block = [x.astype(BF16) for x in (e_t, f_t, g_t, h_t, p_t, d_t, k_t)]
    for i, part in enumerate(block):
        z_ref[pl.ds(i * modes, part.shape[0]), :] = part
    if last:
        side = place(stride * radix, 2)[0] == 1
        send = refs[radix + 6]
        send[pl.ds(0, modes), :] = jnp.where(side, block[2].astype(F32), block[0].astype(F32)).astype(BF16)
        send[pl.ds(modes, modes), :] = jnp.where(side, block[3].astype(F32), block[1].astype(F32)).astype(BF16)
        for i, part in enumerate(block[4:]):
            send[pl.ds((2 + i) * modes, part.shape[0]), :] = part


def finish_kernel(
    stride,
    own_ref, got_ref, dec_t_ref, roots_ref, ratio_ref, scale_ref, fwd_ref, bwd_ref,
    k_ref, v_ref, u_ref, dq_old, dk_old, dv_old,
    dq_hbm, dk_hbm, dv_hbm, dres_hbm, ddec_hbm, dskip_hbm,
    dq_ref, dk_ref, dv_ref, dres_ref, ddec_ref, dskip_ref, total_ref, w_ref, c_ref, sems,
):
    rows, width = k_ref.shape
    modes = dec_t_ref.shape[0]
    steps = rows // SEGS
    tiles = width // LANES
    right = place(stride, 2)[0] == 1
    outs = ((dq_old, dq_ref, dq_hbm), (dk_old, dk_ref, dk_hbm), (dv_old, dv_ref, dv_hbm))

    @pl.when(right)
    def _():
        fetch(sems, *[(old, hbm) for old, _, hbm in outs[1:]])

    @pl.when(jnp.logical_not(right))
    def _():
        fetch(sems, *[(old, hbm) for old, _, hbm in outs[:1]])

    def half(ref, i, n=modes):
        return ref[pl.ds(i * modes, n), :].astype(F32)

    got = half(got_ref, 0), half(got_ref, 1)
    e_l, g_r = jnp.where(right, got[0], half(own_ref, 0)), jnp.where(right, half(own_ref, 2), got[0])
    f_l, h_r = jnp.where(right, got[1], half(own_ref, 1)), jnp.where(right, half(own_ref, 3), got[1])
    proj = half(own_ref, 4) + half(got_ref, 2) + e_l * g_r
    diff = half(own_ref, 5) + half(got_ref, 3) + (f_l * g_r + e_l * h_r)
    dres_ref[...] = roots_ref[...] * proj
    ddec_ref[...] = ratio_ref[...] * diff
    dskip_ref[...] = (half(own_ref, 6, 8) + half(got_ref, 4, 8))[:1]
    copies = fetch(sems, (dres_ref, dres_hbm), (ddec_ref, ddec_hbm), (dskip_ref, dskip_hbm), first=2)
    w_ref[...] = jnp.exp(-dec_t_ref[...])
    c_ref[...] = got[0]

    def add(local_ref, order):
        def one(i, _):
            ln = lanes_of(i)

            def spread(ref, m):
                return jnp.broadcast_to(ref[pl.ds(m, 1), ln], (SEGS, LANES))

            w = [spread(w_ref, m) for m in range(modes)]
            c = [scale_ref[i, pl.ds(m * SEGS, SEGS), :] * spread(c_ref, m) for m in range(modes)]
            for n, j in enumerate(order):
                here = pl.ds(j * SEGS, SEGS)
                y = local_ref[i, here, :]
                for m in range(modes):
                    y = y + c[m]
                    if n < steps - 1:
                        c[m] = c[m] * w[m]
                total_ref[i, here, :] = y
            return 0

        lax.fori_loop(0, tiles, one, 0)

    def rest(work, pairs):
        for seg in range(SEGS):
            for part in range(steps // 16):
                to, frm = rows_in(seg, part, steps)
                for i in range(tiles):
                    work(i, frm, to, pl.ds(i * LANES, LANES))
        done = fetch(sems, *pairs, first=5)
        for copy in done:
            copy.wait()

    @pl.when(right)
    def _():
        add(fwd_ref, range(steps))
        rest(
            lambda i, frm, to, ln: query_rows(u_ref, total_ref, dq_ref, i, frm, to, ln),
            [(new, hbm) for _, new, hbm in outs[:1]],
        )
        for i, (old, _, hbm) in enumerate(outs[1:]):
            pltpu.make_async_copy(old, hbm, sems.at[i]).wait()

    @pl.when(jnp.logical_not(right))
    def _():
        add(bwd_ref, range(steps - 1, -1, -1))
        rest(
            lambda i, frm, to, ln: pair_rows(k_ref, v_ref, total_ref, dk_ref, dv_ref, i, frm, to, ln),
            [(new, hbm) for _, new, hbm in outs[1:]],
        )
        pltpu.make_async_copy(dq_old, dq_hbm, sems.at[0]).wait()

    for copy in copies:
        copy.wait()


def kept(array, space=VMEM):
    return pltpu.with_memory_space_constraint(array, space)


def call(kernel, outs, args, scratch=(), flops=0, name=None, hbm=0, out_space=VMEM):
    return pl.pallas_call(
        kernel,
        out_shape=outs,
        in_specs=[pl.BlockSpec(memory_space=pltpu.HBM)] * hbm + [pl.BlockSpec(memory_space=VMEM)] * (len(args) - hbm),
        out_specs=[pl.BlockSpec(memory_space=out_space)] * len(outs),
        scratch_shapes=list(scratch),
        cost_estimate=pl.CostEstimate(flops=flops, bytes_accessed=1 << 19, transcendentals=0),
        compiler_params=pltpu.CompilerParams(vmem_limit_bytes=24 << 20),
        name=name,
    )(*[kept(a, pltpu.HBM) for a in args[:hbm]], *[kept(a) for a in args[hbm:]])


def exchange(array, mask, size):
    return lax.ppermute(array, "seq", [(i, i ^ mask) for i in range(size)])


def shards(queries, keys, values, upstream, residues, decay, skip):
    rows, width = queries.shape
    modes = residues.shape[1]
    size = lax.axis_size("seq")
    seg_rows = modes * SEGS
    z_rows = 6 * modes + 8
    tiles = width // LANES
    big = VMEM((tiles, rows, LANES), F32)
    state = VMEM((modes, width), F32)
    spread = VMEM((tiles, seg_rows, LANES), F32)
    block = VMEM((z_rows, width), BF16)
    local = VMEM((rows, width), BF16)
    z, gated, grad, pre, post, dec_t, keys, values, upstream, queries = call(
        summary_kernel,
        [block, big, big, spread, spread, state] + [local] * 4,
        [decay.T, keys, values, upstream, queries],
        [spread] * 7 + [pltpu.SemaphoreType.DMA((1 + 4 * tiles,))],
        flops=12 * rows * width * modes,
        name="summary",
        hbm=5,
    )
    s = r = jnp.zeros((modes, width), F32)
    for stride in (1, 4):
        parts = [z] + [exchange(z, k * stride, size) for k in (1, 3, 2)]
        z, s, r = call(
            functools.partial(four_kernel, stride, rows),
            [block, state, state],
            [*parts, dec_t, s, r],
            name=f"combine{stride}",
        )
    z, s, r, send = call(
        functools.partial(combine_kernel, 16, 2, rows, True),
        [block, state, state, VMEM((4 * modes + 8, width), BF16)],
        [z, exchange(z, 16, size), dec_t, s, r],
        name="combine16",
    )
    got = exchange(send, 48, size)
    fwd, bwd, scale, roots, ratio, dq, dk, dv = call(
        functools.partial(conv_kernel, 32, rows),
        [big, big, spread, state, state] + [local] * 3,
        [residues.T, skip.reshape(1, width), gated, grad, dec_t, pre, post, s, r, keys, values, upstream],
        [state, VMEM((1, width), F32)] + [spread] * 4 + [pltpu.SemaphoreType.DMA((2,))],
        flops=8 * rows * width * modes,
        name="conv",
        hbm=2,
    )
    outs = [jax.ShapeDtypeStruct((rows, width), BF16)] * 3
    outs += [jax.ShapeDtypeStruct((modes, width), F32)] * 2
    outs += [jax.ShapeDtypeStruct((1, width), F32)]
    dq, dk, dv, dres, ddec, dskip = call(
        functools.partial(finish_kernel, 32),
        outs,
        [z, got, dec_t, roots, ratio, scale, fwd, bwd, keys, values, upstream, dq, dk, dv],
        [local] * 3 + [state] * 2 + [VMEM((1, width), F32), big, state, state, pltpu.SemaphoreType.DMA((7,))],
        name="finish",
        out_space=pltpu.HBM,
    )
    return dq, dk, dv, dres.T, ddec.T, dskip.reshape(width)


def solution(mesh):
    tokens = P("seq", "chan")
    return jax.shard_map(
        shards,
        mesh=mesh,
        in_specs=(tokens, tokens, tokens, tokens, P("chan", None), P("chan", None), P("chan")),
        out_specs=(tokens, tokens, tokens, P("chan", None), P("chan", None), P("chan")),
        check_vma=False,
    )
```

```python
import functools

import jax
import jax.numpy as jnp
from jax import lax
from jax.experimental import pallas as pl
from jax.experimental.pallas import tpu as pltpu
from jax.sharding import PartitionSpec as P

F32 = jnp.float32
BF16 = jnp.bfloat16
VMEM = pltpu.VMEM
SEGS = 8
LANES = 128
GROUP = 4
STEP = 8
PAIR = 2


def product(a, b):
    return (a.astype(F32) * b.astype(F32)).astype(BF16).astype(F32)


def lanes_of(i):
    return pl.ds(pl.multiple_of(i * LANES, LANES), LANES)


def rows_of(i, n):
    return pl.ds(pl.multiple_of(i * n, n), n)


def fetch(sems, *pairs, first=0):
    copies = [pltpu.make_async_copy(a, b, sems.at[first + i]) for i, (a, b) in enumerate(pairs)]
    for copy in copies:
        copy.start()
    return copies


def summary_kernel(
    dec_hbm, k_hbm, v_hbm, u_hbm, q_hbm,
    z_ref, gated_ref, grad_ref, pre_ref, post_ref, dec_t_ref, k_ref, v_ref, u_ref, q_ref,
    w_ref, e_ref, e1_ref, g_ref, g1_ref, p_ref, t_ref, sems,
):
    rows, width = q_ref.shape
    modes = dec_t_ref.shape[0]
    steps = rows // SEGS
    tiles = width // LANES
    columns = [pl.ds(i * LANES, LANES) for i in range(tiles)]
    pairs = [(dec_hbm, dec_t_ref)]
    for ln in columns:
        pairs += [(a.at[:, ln], b.at[:, ln]) for a, b in ((k_hbm, k_ref), (v_hbm, v_ref), (u_hbm, u_ref), (q_hbm, q_ref))]
    copies = fetch(sems, *pairs)
    copies[0].wait()
    dec_t = dec_t_ref[...]
    w_all = jnp.exp(-dec_t)
    for i in range(tiles):
        for m in range(modes):
            row = w_all[m : m + 1, i * LANES : (i + 1) * LANES]
            w_ref[i, pl.ds(m * SEGS, SEGS), :] = jnp.broadcast_to(row, (SEGS, LANES))

    blocks = range(0, steps, STEP)

    def lag_sums(i):
        lags = [None] * STEP
        for first in blocks:
            x = [gated_ref[i, pl.ds((first + j) * SEGS, SEGS), :] for j in range(STEP)]
            y = [grad_ref[i, pl.ds((first + j) * SEGS, SEGS), :] for j in range(STEP)]
            for j in range(STEP):
                for back in range(j + 1):
                    term = y[j] * x[j - back]
                    lags[back] = term if lags[back] is None else lags[back] + term
        return lags

    def weighted(low, w):
        part = w[STEP - 2] * low[STEP - 1]
        slope = part
        for j in range(STEP - 2, 0, -1):
            part = part + w[j - 1] * low[j]
            slope = slope + part
        return part + low[0], slope

    def one(base, i, lags):
        at = [pl.ds((base * PAIR + m) * SEGS, SEGS) for m in range(PAIR)]
        w = [[w_ref[i, a, :]] for a in at]
        for powers in w:
            for j in range(1, STEP):
                powers.append(powers[0] * powers[j - 1])
        zero = jnp.zeros((SEGS, LANES), F32)
        h, h1, p, t, g, g1, below, power = ([zero] * PAIR for _ in range(8))
        for first in blocks:
            x = [gated_ref[i, pl.ds((first + j) * SEGS, SEGS), :] for j in range(STEP)]
            y = [grad_ref[i, pl.ds((first + j) * SEGS, SEGS), :] for j in range(STEP)]
            for m in range(PAIR):
                into, into1 = weighted(x[::-1], w[m])
                out, out1 = weighted(y, w[m])
                if first == 0:
                    h[m], h1[m], g[m], g1[m], power[m] = into, into1, out, out1, w[m][-1]
                    continue
                p[m] = p[m] + h[m] * out
                t[m] = t[m] + (h1[m] * out + h[m] * out1)
                wh = w[m][-1] * h[m]
                h1[m] = (w[m][-1] * h1[m] + float(STEP) * wh) + into1
                h[m] = wh + into
                below[m] = below[m] + g[m]
                g[m] = g[m] + power[m] * out
                g1[m] = g1[m] + power[m] * out1
                if first + STEP < steps:
                    power[m] = power[m] * w[m][-1]
        for m in range(PAIR):
            inside, inside1 = weighted(lags, w[m])
            e_ref[i, at[m], :] = w[m][0] * h[m]
            e1_ref[i, at[m], :] = w[m][0] * (h1[m] + h[m])
            g_ref[i, at[m], :] = g[m]
            g1_ref[i, at[m], :] = g1[m] + float(STEP) * (float(len(blocks) - 1) * g[m] - below[m])
            p_ref[i, at[m], :] = w[m][0] * p[m] + inside
            t_ref[i, at[m], :] = w[m][0] * (t[m] + p[m]) + inside1

    for i, ln in enumerate(columns):
        for copy in copies[1 + 4 * i : 5 + 4 * i]:
            copy.wait()
        for seg in range(SEGS):
            for part in range(steps // 16):
                at = pl.ds(seg * steps + part * 16, 16)
                to = pl.ds(part * 16 * SEGS + seg, 16, stride=SEGS)
                gated_ref[i, to, :] = product(k_ref[at, ln], v_ref[at, ln])
                grad_ref[i, to, :] = product(u_ref[at, ln], q_ref[at, ln])
        lags = lag_sums(i)
        skip = jnp.sum(lags[0], axis=0, keepdims=True)
        z_ref[6 * modes :, ln] = jnp.broadcast_to(skip, (8, LANES)).astype(BF16)
        for base in range(modes // PAIR):
            one(base, i, lags)

    for i in range(tiles):
        ln = slice(i * LANES, (i + 1) * LANES)
        dec = dec_t[:, ln]
        w_seg = jnp.exp(dec * (-float(steps)))
        zero = jnp.zeros((modes, LANES), F32)
        s, s1, p, t = zero, zero, zero, zero
        for seg in range(SEGS):
            at = pl.ds(seg, modes, stride=SEGS)
            g, g1 = g_ref[i, at, :], g1_ref[i, at, :]
            pre_ref[i, at, :] = s
            p = p + p_ref[i, at, :] + s * g
            t = t + t_ref[i, at, :] + s1 * g + s * g1
            s1 = w_seg * (s1 + float(steps) * s) + e1_ref[i, at, :]
            s = w_seg * s + e_ref[i, at, :]
        r, r1 = zero, zero
        for seg in range(SEGS - 1, -1, -1):
            at = pl.ds(seg, modes, stride=SEGS)
            post_ref[i, at, :] = r
            r1 = w_seg * (r1 + float(steps) * r) + g1_ref[i, at, :]
            r = w_seg * r + g_ref[i, at, :]
        parts = (s, 0.25 * s - dec * s1, r, 0.25 * r - dec * r1, p, 0.5 * p - dec * t)
        for n, part in enumerate(parts):
            z_ref[n * modes : (n + 1) * modes, ln] = part.astype(BF16)


def place(stride, radix):
    at = lax.axis_index("seq")
    return lax.rem(lax.div(at, stride), radix), lax.rem(at, stride)


def conv_kernel(
    res_hbm, skip_hbm, gated_ref, grad_ref, dec_t_ref, pre_ref, post_ref,
    fwd_ref, bwd_ref, in_ref, out_ref, roots_ref, ratio_ref,
    res_t_ref, skip_ref, w_ref, a_ref, sems,
):
    copies = fetch(sems, (res_hbm, res_t_ref), (skip_hbm, skip_ref))
    tiles, rows, _ = gated_ref.shape
    modes = dec_t_ref.shape[0]
    steps = rows // SEGS
    for copy in copies:
        copy.wait()
    dec_t = dec_t_ref[...]
    roots = jnp.sqrt(dec_t)
    scale = res_t_ref[...] * roots
    roots_ref[...] = roots
    ratio_ref[...] = res_t_ref[...] / roots
    seg_at = lax.broadcasted_iota(jnp.int32, (SEGS, LANES), 0).astype(F32) * float(steps)
    for i in range(tiles):
        ln = slice(i * LANES, (i + 1) * LANES)
        for m in range(modes):
            at = pl.ds(m * SEGS, SEGS)
            d = jnp.broadcast_to(dec_t[m : m + 1, ln], (SEGS, LANES))
            a = jnp.broadcast_to(scale[m : m + 1, ln], (SEGS, LANES))
            w_ref[i, at, :] = jnp.exp(-d)
            a_ref[i, at, :] = a
            in_ref[i, at, :] = a * jnp.exp(-d * seg_at)
            out_ref[i, at, :] = a * jnp.exp(-d * (float(rows - steps + 1) - seg_at))

    def one(i, _):
        direct = jnp.broadcast_to(skip_ref[:, lanes_of(i)], (SEGS, LANES))
        for base in range(0, modes, GROUP):
            at = [pl.ds((base + m) * SEGS, SEGS) for m in range(GROUP)]
            w = [w_ref[i, x, :] for x in at]
            a = [a_ref[i, x, :] for x in at]
            h = [pre_ref[i, x, :] for x in at]
            r = [post_ref[i, x, :] for x in at]
            for j in range(steps):
                at_f = pl.ds(j * SEGS, SEGS)
                at_b = pl.ds((steps - 1 - j) * SEGS, SEGS)
                x, y = gated_ref[i, at_f, :], grad_ref[i, at_b, :]
                f = fwd_ref[i, at_f, :] if base else direct * x
                b = bwd_ref[i, at_b, :] if base else direct * y
                for m in range(GROUP):
                    h[m] = (w[m] * h[m] if j else h[m]) + x
                    r[m] = w[m] * r[m] + y
                    f = f + a[m] * h[m]
                    b = b + a[m] * r[m]
                fwd_ref[i, at_f, :] = f
                bwd_ref[i, at_b, :] = b
        return 0

    lax.fori_loop(0, tiles, one, 0)


def rows_in(seg, part, steps):
    return pl.ds(seg * steps + part * 16, 16), pl.ds(part * 16 * SEGS + seg, 16, stride=SEGS)


def query_rows(u_ref, total_ref, dq_ref, i, frm, to, ln):
    conv = total_ref[i, frm, :].astype(BF16).astype(F32)
    dq_ref[to, ln] = (u_ref[to, ln].astype(F32) * conv).astype(BF16)


def pair_rows(k_ref, v_ref, total_ref, dk_ref, dv_ref, i, frm, to, ln):
    gg = total_ref[i, frm, :].astype(BF16).astype(F32)
    dk_ref[to, ln] = (gg * v_ref[to, ln].astype(F32)).astype(BF16)
    dv_ref[to, ln] = (gg * k_ref[to, ln].astype(F32)).astype(BF16)


def add_state(local_ref, total_ref, scale_ref, state_ref, w_ref, order, tiles, modes):
    def one(i, _):
        ln = lanes_of(i)

        def spread(ref, m):
            return jnp.broadcast_to(ref[pl.ds(m, 1), ln], (SEGS, LANES))

        w = [spread(w_ref, m) for m in range(modes)]
        c = [scale_ref[i, pl.ds(m * SEGS, SEGS), :] * spread(state_ref, m) for m in range(modes)]
        for n, j in enumerate(order):
            here = pl.ds(j * SEGS, SEGS)
            y = local_ref[i, here, :]
            for m in range(modes):
                y = y + c[m]
                if n < len(order) - 1:
                    c[m] = c[m] * w[m]
            total_ref[i, here, :] = y
        return 0

    lax.fori_loop(0, tiles, one, 0)


def known_kernel(
    stride, count,
    dec_t_ref, s_ref, r_ref, in_ref, out_ref, fwd_old, bwd_old, k_ref, v_ref, u_ref,
    fwd_ref, bwd_ref, far_ref, w_ref, dq_ref, dk_ref, dv_ref,
):
    tiles, rows, _ = fwd_ref.shape
    modes = dec_t_ref.shape[0]
    steps = rows // SEGS
    digit, offset = place(stride, 2)
    chunks = jnp.where(digit == 1, offset, stride - 1 - offset).astype(F32)
    dec_t = dec_t_ref[...]
    far_ref[...] = jnp.exp(dec_t * (-float(count) * chunks))
    w_ref[...] = jnp.exp(-dec_t)
    add_state(fwd_old, fwd_ref, in_ref, s_ref, w_ref, range(steps), tiles, modes)
    add_state(bwd_old, bwd_ref, out_ref, r_ref, w_ref, range(steps - 1, -1, -1), tiles, modes)
    for seg in range(SEGS):
        for part in range(steps // 16):
            to, frm = rows_in(seg, part, steps)
            for i in range(tiles):
                ln = pl.ds(i * LANES, LANES)
                query_rows(u_ref, fwd_ref, dq_ref, i, frm, to, ln)
                pair_rows(k_ref, v_ref, bwd_ref, dk_ref, dv_ref, i, frm, to, ln)


def four_kernel(stride, count, z0, z1, z3, z2, dec_t_ref, s_ref, r_ref, *refs):
    combine_kernel(stride, 4, count, False, z0, z1, z2, z3, dec_t_ref, s_ref, r_ref, *refs[-3:])


def combine_kernel(stride, radix, count, last, *refs):
    parts = refs[:radix]
    dec_t_ref, s_ref, r_ref, z_ref, s_out, r_out = refs[radix : radix + 6]
    dec_t = dec_t_ref[...]
    modes = dec_t.shape[0]
    digit, offset = place(stride, radix)
    offset = offset.astype(F32)

    def gather(i, n=modes):
        have = [part[pl.ds(i * modes, n), :].astype(F32) for part in parts]
        pick = []
        for j in range(radix):
            k = digit ^ j
            first = jnp.where(k == 0, have[0], have[1])
            if radix == 4:
                first = jnp.where(k >= 2, jnp.where(k == 2, have[2], have[3]), first)
            pick.append(first)
        return pick

    e, f, g, h, p, d = (gather(i) for i in range(6))
    k = gather(6, 8)
    one = dec_t * float(count * stride)
    w = [jnp.exp(one * (-float(j))) for j in range(radix)]
    e_t, f_t, g_t, h_t, p_t, d_t, k_t = e[0], f[0], g[0], h[0], p[0], d[0], k[0]
    enter = jnp.zeros_like(dec_t)
    for j in range(1, radix):
        enter = jnp.where(digit == j, e_t, enter)
        p_t = p_t + p[j] + e_t * g[j]
        d_t = d_t + d[j] + f_t * g[j] + e_t * h[j]
        f_t = w[1] * (f_t - one * e_t) + f[j]
        e_t = w[1] * e_t + e[j]
        h_t = h_t + w[j] * (h[j] - one * float(j) * g[j])
        g_t = g_t + w[j] * g[j]
        k_t = k_t + k[j]
    leave = jnp.zeros_like(dec_t)
    tail = g[-1]
    for j in range(radix - 2, -1, -1):
        leave = jnp.where(digit == j, tail, leave)
        tail = g[j] + w[1] * tail
    s_out[...] = s_ref[...] + jnp.exp(dec_t * (-float(count) * offset)) * enter
    r_out[...] = r_ref[...] + jnp.exp(dec_t * (-float(count) * (float(stride - 1) - offset))) * leave
    block = [x.astype(BF16) for x in (e_t, f_t, g_t, h_t, p_t, d_t, k_t)]
    for i, part in enumerate(block):
        z_ref[pl.ds(i * modes, part.shape[0]), :] = part
    if last:
        side = place(stride * radix, 2)[0] == 1
        send = refs[radix + 6]
        send[pl.ds(0, modes), :] = jnp.where(side, block[2].astype(F32), block[0].astype(F32)).astype(BF16)
        send[pl.ds(modes, modes), :] = jnp.where(side, block[3].astype(F32), block[1].astype(F32)).astype(BF16)
        for i, part in enumerate(block[4:]):
            send[pl.ds((2 + i) * modes, part.shape[0]), :] = part


def finish_kernel(
    stride,
    own_ref, got_ref, roots_ref, ratio_ref, in_ref, out_ref, far_ref, w_ref, fwd_ref, bwd_ref,
    k_ref, v_ref, u_ref, dq_old, dk_old, dv_old,
    dq_hbm, dk_hbm, dv_hbm, dres_hbm, ddec_hbm, dskip_hbm,
    dq_ref, dk_ref, dv_ref, dres_ref, ddec_ref, dskip_ref, total_ref, c_ref, sems,
):
    rows, width = k_ref.shape
    modes = w_ref.shape[0]
    steps = rows // SEGS
    tiles = width // LANES
    right = place(stride, 2)[0] == 1
    outs = ((dq_old, dq_ref, dq_hbm), (dk_old, dk_ref, dk_hbm), (dv_old, dv_ref, dv_hbm))

    @pl.when(right)
    def _():
        fetch(sems, *[(old, hbm) for old, _, hbm in outs[1:]])

    @pl.when(jnp.logical_not(right))
    def _():
        fetch(sems, *[(old, hbm) for old, _, hbm in outs[:1]])

    def half(ref, i, n=modes):
        return ref[pl.ds(i * modes, n), :].astype(F32)

    got = half(got_ref, 0), half(got_ref, 1)
    e_l, g_r = jnp.where(right, got[0], half(own_ref, 0)), jnp.where(right, half(own_ref, 2), got[0])
    f_l, h_r = jnp.where(right, got[1], half(own_ref, 1)), jnp.where(right, half(own_ref, 3), got[1])
    proj = half(own_ref, 4) + half(got_ref, 2) + e_l * g_r
    diff = half(own_ref, 5) + half(got_ref, 3) + (f_l * g_r + e_l * h_r)
    dres_ref[...] = roots_ref[...] * proj
    ddec_ref[...] = ratio_ref[...] * diff
    dskip_ref[...] = (half(own_ref, 6, 8) + half(got_ref, 4, 8))[:1]
    copies = fetch(sems, (dres_ref, dres_hbm), (ddec_ref, ddec_hbm), (dskip_ref, dskip_hbm), first=2)
    c_ref[...] = got[0] * far_ref[...]

    def rest(work, pairs):
        for seg in range(SEGS):
            for part in range(steps // 16):
                to, frm = rows_in(seg, part, steps)
                for i in range(tiles):
                    work(i, frm, to, pl.ds(i * LANES, LANES))
        done = fetch(sems, *pairs, first=5)
        for copy in done:
            copy.wait()

    @pl.when(right)
    def _():
        add_state(fwd_ref, total_ref, in_ref, c_ref, w_ref, range(steps), tiles, modes)
        rest(
            lambda i, frm, to, ln: query_rows(u_ref, total_ref, dq_ref, i, frm, to, ln),
            [(new, hbm) for _, new, hbm in outs[:1]],
        )
        for i, (old, _, hbm) in enumerate(outs[1:]):
            pltpu.make_async_copy(old, hbm, sems.at[i]).wait()

    @pl.when(jnp.logical_not(right))
    def _():
        add_state(bwd_ref, total_ref, out_ref, c_ref, w_ref, range(steps - 1, -1, -1), tiles, modes)
        rest(
            lambda i, frm, to, ln: pair_rows(k_ref, v_ref, total_ref, dk_ref, dv_ref, i, frm, to, ln),
            [(new, hbm) for _, new, hbm in outs[1:]],
        )
        pltpu.make_async_copy(dq_old, dq_hbm, sems.at[0]).wait()

    for copy in copies:
        copy.wait()


def kept(array, space=VMEM):
    return pltpu.with_memory_space_constraint(array, space)


def call(kernel, outs, args, scratch=(), flops=0, name=None, hbm=0, out_space=VMEM):
    return pl.pallas_call(
        kernel,
        out_shape=outs,
        in_specs=[pl.BlockSpec(memory_space=pltpu.HBM)] * hbm + [pl.BlockSpec(memory_space=VMEM)] * (len(args) - hbm),
        out_specs=[pl.BlockSpec(memory_space=out_space)] * len(outs),
        scratch_shapes=list(scratch),
        cost_estimate=pl.CostEstimate(flops=flops, bytes_accessed=1 << 19, transcendentals=0),
        compiler_params=pltpu.CompilerParams(vmem_limit_bytes=24 << 20),
        name=name,
    )(*[kept(a, pltpu.HBM) for a in args[:hbm]], *[kept(a) for a in args[hbm:]])


def exchange(array, mask, size):
    return lax.ppermute(array, "seq", [(i, i ^ mask) for i in range(size)])


def shards(queries, keys, values, upstream, residues, decay, skip):
    rows, width = queries.shape
    modes = residues.shape[1]
    size = lax.axis_size("seq")
    seg_rows = modes * SEGS
    z_rows = 6 * modes + 8
    tiles = width // LANES
    big = VMEM((tiles, rows, LANES), F32)
    state = VMEM((modes, width), F32)
    spread = VMEM((tiles, seg_rows, LANES), F32)
    block = VMEM((z_rows, width), BF16)
    local = VMEM((rows, width), BF16)
    z, gated, grad, pre, post, dec_t, keys, values, upstream, queries = call(
        summary_kernel,
        [block, big, big, spread, spread, state] + [local] * 4,
        [decay.T, keys, values, upstream, queries],
        [spread] * 7 + [pltpu.SemaphoreType.DMA((1 + 4 * tiles,))],
        flops=12 * rows * width * modes,
        name="summary",
        hbm=5,
    )
    fwd, bwd, in_w, out_w, roots, ratio = call(
        conv_kernel,
        [big, big, spread, spread, state, state],
        [residues.T, skip.reshape(1, width), gated, grad, dec_t, pre, post],
        [state, VMEM((1, width), F32)] + [spread] * 2 + [pltpu.SemaphoreType.DMA((2,))],
        flops=8 * rows * width * modes,
        name="conv",
        hbm=2,
    )
    s = r = jnp.zeros((modes, width), F32)
    for stride in (1, 4):
        parts = [z] + [exchange(z, k * stride, size) for k in (1, 3, 2)]
        z, s, r = call(
            functools.partial(four_kernel, stride, rows),
            [block, state, state],
            [*parts, dec_t, s, r] + [roots] * (stride == 1),
            name=f"combine{stride}",
        )
    z, s, r, send = call(
        functools.partial(combine_kernel, 16, 2, rows, True),
        [block, state, state, VMEM((4 * modes + 8, width), BF16)],
        [z, exchange(z, 16, size), dec_t, s, r],
        name="combine16",
    )
    got = exchange(send, 48, size)
    fwd, bwd, far, w, dq, dk, dv = call(
        functools.partial(known_kernel, 32, rows),
        [big, big, state, state] + [local] * 3,
        [dec_t, s, r, in_w, out_w, fwd, bwd, keys, values, upstream],
        flops=4 * rows * width * modes,
        name="known",
    )
    outs = [jax.ShapeDtypeStruct((rows, width), BF16)] * 3
    outs += [jax.ShapeDtypeStruct((modes, width), F32)] * 2
    outs += [jax.ShapeDtypeStruct((1, width), F32)]
    dq, dk, dv, dres, ddec, dskip = call(
        functools.partial(finish_kernel, 32),
        outs,
        [z, got, roots, ratio, in_w, out_w, far, w, fwd, bwd, keys, values, upstream, dq, dk, dv],
        [local] * 3 + [state] * 2 + [VMEM((1, width), F32), big, state, pltpu.SemaphoreType.DMA((7,))],
        name="finish",
        out_space=pltpu.HBM,
    )
    return dq, dk, dv, dres.T, ddec.T, dskip.reshape(width)


def solution(mesh):
    tokens = P("seq", "chan")
    return jax.shard_map(
        shards,
        mesh=mesh,
        in_specs=(tokens, tokens, tokens, tokens, P("chan", None), P("chan", None), P("chan")),
        out_specs=(tokens, tokens, tokens, P("chan", None), P("chan", None), P("chan")),
        check_vma=False,
    )
```

```python
import functools

import jax
import jax.numpy as jnp
from jax import lax
from jax.experimental import pallas as pl
from jax.experimental.pallas import tpu as pltpu
from jax.sharding import PartitionSpec as P

F32 = jnp.float32
BF16 = jnp.bfloat16
VMEM = pltpu.VMEM
SEGS = 8
LANES = 128
GROUP = 4
STEP = 8
PAIR = 2


def product(a, b):
    return (a.astype(F32) * b.astype(F32)).astype(BF16).astype(F32)


def lanes_of(i):
    return pl.ds(pl.multiple_of(i * LANES, LANES), LANES)


def rows_of(i, n):
    return pl.ds(pl.multiple_of(i * n, n), n)


def fetch(sems, *pairs, first=0):
    copies = [pltpu.make_async_copy(a, b, sems.at[first + i]) for i, (a, b) in enumerate(pairs)]
    for copy in copies:
        copy.start()
    return copies


def summary_kernel(
    dec_hbm, k_hbm, v_hbm, u_hbm, q_hbm,
    z_ref, gated_ref, grad_ref, pre_ref, post_ref, dec_t_ref, k_ref, v_ref, u_ref, q_ref,
    w_ref, e_ref, e1_ref, g_ref, g1_ref, p_ref, t_ref, sems,
):
    rows, width = q_ref.shape
    modes = dec_t_ref.shape[0]
    steps = rows // SEGS
    tiles = width // LANES
    columns = [pl.ds(i * LANES, LANES) for i in range(tiles)]
    pairs = [(dec_hbm, dec_t_ref)]
    for ln in columns:
        pairs += [(a.at[:, ln], b.at[:, ln]) for a, b in ((k_hbm, k_ref), (v_hbm, v_ref), (u_hbm, u_ref), (q_hbm, q_ref))]
    copies = fetch(sems, *pairs)
    copies[0].wait()
    dec_t = dec_t_ref[...]
    w_all = jnp.exp(-dec_t)
    for i in range(tiles):
        for m in range(modes):
            row = w_all[m : m + 1, i * LANES : (i + 1) * LANES]
            w_ref[i, pl.ds(m * SEGS, SEGS), :] = jnp.broadcast_to(row, (SEGS, LANES))

    blocks = range(0, steps, STEP)

    def lag_sums(i):
        lags = [None] * STEP
        for first in blocks:
            x = [gated_ref[i, pl.ds((first + j) * SEGS, SEGS), :] for j in range(STEP)]
            y = [grad_ref[i, pl.ds((first + j) * SEGS, SEGS), :] for j in range(STEP)]
            for j in range(STEP):
                for back in range(j + 1):
                    term = y[j] * x[j - back]
                    lags[back] = term if lags[back] is None else lags[back] + term
        return lags

    def weighted(low, w):
        part = w[STEP - 2] * low[STEP - 1]
        slope = part
        for j in range(STEP - 2, 0, -1):
            part = part + w[j - 1] * low[j]
            slope = slope + part
        return part + low[0], slope

    def one(base, i, lags):
        at = [pl.ds((base * PAIR + m) * SEGS, SEGS) for m in range(PAIR)]
        w = [[w_ref[i, a, :]] for a in at]
        for powers in w:
            for j in range(1, STEP):
                powers.append(powers[0] * powers[j - 1])
        zero = jnp.zeros((SEGS, LANES), F32)
        h, h1, p, t, g, g1, below, power = ([zero] * PAIR for _ in range(8))
        for first in blocks:
            x = [gated_ref[i, pl.ds((first + j) * SEGS, SEGS), :] for j in range(STEP)]
            y = [grad_ref[i, pl.ds((first + j) * SEGS, SEGS), :] for j in range(STEP)]
            for m in range(PAIR):
                into, into1 = weighted(x[::-1], w[m])
                out, out1 = weighted(y, w[m])
                if first == 0:
                    h[m], h1[m], g[m], g1[m], power[m] = into, into1, out, out1, w[m][-1]
                    continue
                p[m] = p[m] + h[m] * out
                t[m] = t[m] + (h1[m] * out + h[m] * out1)
                wh = w[m][-1] * h[m]
                h1[m] = (w[m][-1] * h1[m] + float(STEP) * wh) + into1
                h[m] = wh + into
                below[m] = below[m] + g[m]
                g[m] = g[m] + power[m] * out
                g1[m] = g1[m] + power[m] * out1
                if first + STEP < steps:
                    power[m] = power[m] * w[m][-1]
        for m in range(PAIR):
            inside, inside1 = weighted(lags, w[m])
            e_ref[i, at[m], :] = w[m][0] * h[m]
            e1_ref[i, at[m], :] = w[m][0] * (h1[m] + h[m])
            g_ref[i, at[m], :] = g[m]
            g1_ref[i, at[m], :] = g1[m] + float(STEP) * (float(len(blocks) - 1) * g[m] - below[m])
            p_ref[i, at[m], :] = w[m][0] * p[m] + inside
            t_ref[i, at[m], :] = w[m][0] * (t[m] + p[m]) + inside1

    for i, ln in enumerate(columns):
        for copy in copies[1 + 4 * i : 5 + 4 * i]:
            copy.wait()
        for seg in range(SEGS):
            for part in range(steps // 16):
                at = pl.ds(seg * steps + part * 16, 16)
                to = pl.ds(part * 16 * SEGS + seg, 16, stride=SEGS)
                gated_ref[i, to, :] = product(k_ref[at, ln], v_ref[at, ln])
                grad_ref[i, to, :] = product(u_ref[at, ln], q_ref[at, ln])
        lags = lag_sums(i)
        skip = jnp.sum(lags[0], axis=0, keepdims=True)
        z_ref[6 * modes :, ln] = jnp.broadcast_to(skip, (8, LANES)).astype(BF16)
        for base in range(modes // PAIR):
            one(base, i, lags)

    for i in range(tiles):
        ln = slice(i * LANES, (i + 1) * LANES)
        dec = dec_t[:, ln]
        w_seg = jnp.exp(dec * (-float(steps)))
        zero = jnp.zeros((modes, LANES), F32)
        s, s1, p, t = zero, zero, zero, zero
        for seg in range(SEGS):
            at = pl.ds(seg, modes, stride=SEGS)
            g, g1 = g_ref[i, at, :], g1_ref[i, at, :]
            pre_ref[i, at, :] = s
            p = p + p_ref[i, at, :] + s * g
            t = t + t_ref[i, at, :] + s1 * g + s * g1
            s1 = w_seg * (s1 + float(steps) * s) + e1_ref[i, at, :]
            s = w_seg * s + e_ref[i, at, :]
        r, r1 = zero, zero
        for seg in range(SEGS - 1, -1, -1):
            at = pl.ds(seg, modes, stride=SEGS)
            post_ref[i, at, :] = r
            r1 = w_seg * (r1 + float(steps) * r) + g1_ref[i, at, :]
            r = w_seg * r + g_ref[i, at, :]
        parts = (s, 0.25 * s - dec * s1, r, 0.25 * r - dec * r1, p, 0.5 * p - dec * t)
        for n, part in enumerate(parts):
            z_ref[n * modes : (n + 1) * modes, ln] = part.astype(BF16)


def place(stride, radix):
    at = lax.axis_index("seq")
    return lax.rem(lax.div(at, stride), radix), lax.rem(at, stride)


def conv_kernel(
    res_hbm, skip_hbm, gated_ref, grad_ref, dec_t_ref, pre_ref, post_ref,
    fwd_ref, bwd_ref, in_ref, out_ref, roots_ref, ratio_ref,
    res_t_ref, skip_ref, w_ref, a_ref, sems,
):
    copies = fetch(sems, (res_hbm, res_t_ref), (skip_hbm, skip_ref))
    tiles, rows, _ = gated_ref.shape
    modes = dec_t_ref.shape[0]
    steps = rows // SEGS
    for copy in copies:
        copy.wait()
    dec_t = dec_t_ref[...]
    roots = jnp.sqrt(dec_t)
    scale = res_t_ref[...] * roots
    roots_ref[...] = roots
    ratio_ref[...] = res_t_ref[...] / roots
    seg_at = lax.broadcasted_iota(jnp.int32, (SEGS, LANES), 0).astype(F32) * float(steps)
    for i in range(tiles):
        ln = slice(i * LANES, (i + 1) * LANES)
        for m in range(modes):
            at = pl.ds(m * SEGS, SEGS)
            d = jnp.broadcast_to(dec_t[m : m + 1, ln], (SEGS, LANES))
            a = jnp.broadcast_to(scale[m : m + 1, ln], (SEGS, LANES))
            w_ref[i, at, :] = jnp.exp(-d)
            a_ref[i, at, :] = a
            in_ref[i, at, :] = a * jnp.exp(-d * seg_at)
            out_ref[i, at, :] = a * jnp.exp(-d * (float(rows - steps + 1) - seg_at))

    def one(i, _):
        direct = jnp.broadcast_to(skip_ref[:, lanes_of(i)], (SEGS, LANES))
        for base in range(0, modes, GROUP):
            at = [pl.ds((base + m) * SEGS, SEGS) for m in range(GROUP)]
            w = [w_ref[i, x, :] for x in at]
            a = [a_ref[i, x, :] for x in at]
            h = [pre_ref[i, x, :] for x in at]
            r = [post_ref[i, x, :] for x in at]
            for j in range(steps):
                at_f = pl.ds(j * SEGS, SEGS)
                at_b = pl.ds((steps - 1 - j) * SEGS, SEGS)
                x, y = gated_ref[i, at_f, :], grad_ref[i, at_b, :]
                f = fwd_ref[i, at_f, :] if base else direct * x
                b = bwd_ref[i, at_b, :] if base else direct * y
                for m in range(GROUP):
                    h[m] = (w[m] * h[m] if j else h[m]) + x
                    r[m] = w[m] * r[m] + y
                    f = f + a[m] * h[m]
                    b = b + a[m] * r[m]
                fwd_ref[i, at_f, :] = f
                bwd_ref[i, at_b, :] = b
        return 0

    lax.fori_loop(0, tiles, one, 0)


def rows_in(seg, part, steps):
    return pl.ds(seg * steps + part * 16, 16), pl.ds(part * 16 * SEGS + seg, 16, stride=SEGS)


def query_rows(u_ref, total_ref, dq_ref, i, frm, to, ln):
    conv = total_ref[i, frm, :].astype(BF16).astype(F32)
    dq_ref[to, ln] = (u_ref[to, ln].astype(F32) * conv).astype(BF16)


def pair_rows(k_ref, v_ref, total_ref, dk_ref, dv_ref, i, frm, to, ln):
    gg = total_ref[i, frm, :].astype(BF16).astype(F32)
    dk_ref[to, ln] = (gg * v_ref[to, ln].astype(F32)).astype(BF16)
    dv_ref[to, ln] = (gg * k_ref[to, ln].astype(F32)).astype(BF16)


def add_state(local_ref, total_ref, scale_ref, state_ref, w_ref, order, tiles, modes):
    def one(i, _):
        ln = lanes_of(i)

        def spread(ref, m):
            return jnp.broadcast_to(ref[pl.ds(m, 1), ln], (SEGS, LANES))

        w = [spread(w_ref, m) for m in range(modes)]
        c = [scale_ref[i, pl.ds(m * SEGS, SEGS), :] * spread(state_ref, m) for m in range(modes)]
        for n, j in enumerate(order):
            here = pl.ds(j * SEGS, SEGS)
            y = local_ref[i, here, :]
            for m in range(modes):
                y = y + c[m]
                if n < len(order) - 1:
                    c[m] = c[m] * w[m]
            total_ref[i, here, :] = y
        return 0

    lax.fori_loop(0, tiles, one, 0)


def known_kernel(
    stride, count,
    pair_ref, dec_t_ref, s_ref, r_ref, in_ref, out_ref, fwd_old, bwd_old, k_ref, v_ref, u_ref,
    fwd_ref, bwd_ref, s_out, r_out, w_ref, dq_ref, dk_ref, dv_ref,
):
    tiles, rows, _ = fwd_ref.shape
    modes = dec_t_ref.shape[0]
    steps = rows // SEGS
    digit, offset = place(stride, 2)
    offset = offset.astype(F32)
    dec_t = dec_t_ref[...]
    enter = jnp.exp(dec_t * (-float(count) * offset)) * pair_ref[pl.ds(0, modes), :].astype(F32)
    leave = jnp.exp(dec_t * (-float(count) * (float(stride - 1) - offset))) * pair_ref[pl.ds(2 * modes, modes), :].astype(F32)
    s_out[...] = s_ref[...] + jnp.where(digit == 1, enter, 0.0)
    r_out[...] = r_ref[...] + jnp.where(digit == 1, 0.0, leave)
    w_ref[...] = jnp.exp(-dec_t)
    add_state(fwd_old, fwd_ref, in_ref, s_out, w_ref, range(steps), tiles, modes)
    add_state(bwd_old, bwd_ref, out_ref, r_out, w_ref, range(steps - 1, -1, -1), tiles, modes)
    for seg in range(SEGS):
        for part in range(steps // 16):
            to, frm = rows_in(seg, part, steps)
            for i in range(tiles):
                ln = pl.ds(i * LANES, LANES)
                query_rows(u_ref, fwd_ref, dq_ref, i, frm, to, ln)
                pair_rows(k_ref, v_ref, bwd_ref, dk_ref, dv_ref, i, frm, to, ln)


def combine(stride, count, parts, dec_t, s, r):
    modes = dec_t.shape[0]
    digit, offset = place(stride, 4)
    offset = offset.astype(F32)

    def gather(i, n=modes):
        have = [parts(k, i, n) for k in range(4)]
        pick = []
        for j in range(4):
            k = digit ^ j
            pick.append(jnp.where(k >= 2, jnp.where(k == 2, have[2], have[3]), jnp.where(k == 0, have[0], have[1])))
        return pick

    e, f, g, h, p, d = (gather(i) for i in range(6))
    k = gather(6, 8)
    one = dec_t * float(count * stride)
    w = [jnp.exp(one * (-float(j))) for j in range(4)]
    e_t, f_t, g_t, h_t, p_t, d_t, k_t = e[0], f[0], g[0], h[0], p[0], d[0], k[0]
    enter = jnp.zeros_like(dec_t)
    for j in range(1, 4):
        enter = jnp.where(digit == j, e_t, enter)
        p_t = p_t + p[j] + e_t * g[j]
        d_t = d_t + d[j] + f_t * g[j] + e_t * h[j]
        f_t = w[1] * (f_t - one * e_t) + f[j]
        e_t = w[1] * e_t + e[j]
        h_t = h_t + w[j] * (h[j] - one * float(j) * g[j])
        g_t = g_t + w[j] * g[j]
        k_t = k_t + k[j]
    leave = jnp.zeros_like(dec_t)
    tail = g[3]
    for j in range(2, -1, -1):
        leave = jnp.where(digit == j, tail, leave)
        tail = g[j] + w[1] * tail
    s = s + jnp.exp(dec_t * (-float(count) * offset)) * enter
    r = r + jnp.exp(dec_t * (-float(count) * (float(stride - 1) - offset))) * leave
    return (e_t, f_t, g_t, h_t, p_t, d_t, k_t), s, r


def combine_kernel(stride, count, z0, z2, z3, z1, dec_t_ref, s_ref, r_ref, *refs):
    z_ref, s_out, r_out = refs[-3:]
    modes = dec_t_ref.shape[0]

    def parts(k, i, n):
        return (z0, z1, z2, z3)[k][pl.ds(i * modes, n), :].astype(F32)

    block, s_out[...], r_out[...] = combine(stride, count, parts, dec_t_ref[...], s_ref[...], r_ref[...])
    for i, part in enumerate(block):
        z_ref[pl.ds(i * modes, part.shape[0]), :] = part.astype(BF16)


def finish_kernel(
    stride, count,
    own_ref, pair_ref, far_ref, near_ref, dec_t_ref, s_ref, r_ref, s_known, r_known,
    roots_ref, ratio_ref, in_ref, out_ref, w_ref, fwd_ref, bwd_ref,
    k_ref, v_ref, u_ref, dq_old, dk_old, dv_old,
    dq_hbm, dk_hbm, dv_hbm, dres_hbm, ddec_hbm, dskip_hbm,
    dq_ref, dk_ref, dv_ref, dres_ref, ddec_ref, dskip_ref, total_ref, c_ref, sems,
):
    rows, width = k_ref.shape
    modes = w_ref.shape[0]
    steps = rows // SEGS
    tiles = width // LANES
    right = place(2 * stride, 2)[0] == 1
    outs = ((dq_old, dq_ref, dq_hbm), (dk_old, dk_ref, dk_hbm), (dv_old, dv_ref, dv_hbm))

    @pl.when(right)
    def _():
        fetch(sems, *[(old, hbm) for old, _, hbm in outs[1:]])

    @pl.when(jnp.logical_not(right))
    def _():
        fetch(sems, *[(old, hbm) for old, _, hbm in outs[:1]])

    def parts(k, i, n):
        return (own_ref, pair_ref, far_ref, near_ref)[k][pl.ds(i * modes, n), :].astype(F32)

    block, s, r = combine(stride, count, parts, dec_t_ref[...], s_ref[...], r_ref[...])
    c_ref[...] = jnp.where(right, s - s_known[...], r - r_known[...])
    dres_ref[...] = roots_ref[...] * block[4]
    ddec_ref[...] = ratio_ref[...] * block[5]
    dskip_ref[...] = block[6][:1]
    copies = fetch(sems, (dres_ref, dres_hbm), (ddec_ref, ddec_hbm), (dskip_ref, dskip_hbm), first=2)

    def rest(work, pairs):
        for seg in range(SEGS):
            for part in range(steps // 16):
                to, frm = rows_in(seg, part, steps)
                for i in range(tiles):
                    work(i, frm, to, pl.ds(i * LANES, LANES))
        done = fetch(sems, *pairs, first=5)
        for copy in done:
            copy.wait()

    @pl.when(right)
    def _():
        add_state(fwd_ref, total_ref, in_ref, c_ref, w_ref, range(steps), tiles, modes)
        rest(
            lambda i, frm, to, ln: query_rows(u_ref, total_ref, dq_ref, i, frm, to, ln),
            [(new, hbm) for _, new, hbm in outs[:1]],
        )
        for i, (old, _, hbm) in enumerate(outs[1:]):
            pltpu.make_async_copy(old, hbm, sems.at[i]).wait()

    @pl.when(jnp.logical_not(right))
    def _():
        add_state(bwd_ref, total_ref, out_ref, c_ref, w_ref, range(steps - 1, -1, -1), tiles, modes)
        rest(
            lambda i, frm, to, ln: pair_rows(k_ref, v_ref, total_ref, dk_ref, dv_ref, i, frm, to, ln),
            [(new, hbm) for _, new, hbm in outs[1:]],
        )
        pltpu.make_async_copy(dq_old, dq_hbm, sems.at[0]).wait()

    for copy in copies:
        copy.wait()


def kept(array, space=VMEM):
    return pltpu.with_memory_space_constraint(array, space)


def call(kernel, outs, args, scratch=(), flops=0, name=None, hbm=0, out_space=VMEM):
    return pl.pallas_call(
        kernel,
        out_shape=outs,
        in_specs=[pl.BlockSpec(memory_space=pltpu.HBM)] * hbm + [pl.BlockSpec(memory_space=VMEM)] * (len(args) - hbm),
        out_specs=[pl.BlockSpec(memory_space=out_space)] * len(outs),
        scratch_shapes=list(scratch),
        cost_estimate=pl.CostEstimate(flops=flops, bytes_accessed=1 << 19, transcendentals=0),
        compiler_params=pltpu.CompilerParams(vmem_limit_bytes=24 << 20),
        name=name,
    )(*[kept(a, pltpu.HBM) for a in args[:hbm]], *[kept(a) for a in args[hbm:]])


def exchange(array, mask, size):
    return lax.ppermute(array, "seq", [(i, i ^ mask) for i in range(size)])


def shards(queries, keys, values, upstream, residues, decay, skip):
    rows, width = queries.shape
    modes = residues.shape[1]
    size = lax.axis_size("seq")
    seg_rows = modes * SEGS
    z_rows = 6 * modes + 8
    tiles = width // LANES
    big = VMEM((tiles, rows, LANES), F32)
    state = VMEM((modes, width), F32)
    spread = VMEM((tiles, seg_rows, LANES), F32)
    block = VMEM((z_rows, width), BF16)
    local = VMEM((rows, width), BF16)
    z, gated, grad, pre, post, dec_t, keys, values, upstream, queries = call(
        summary_kernel,
        [block, big, big, spread, spread, state] + [local] * 4,
        [decay.T, keys, values, upstream, queries],
        [spread] * 7 + [pltpu.SemaphoreType.DMA((1 + 4 * tiles,))],
        flops=12 * rows * width * modes,
        name="summary",
        hbm=5,
    )
    fwd, bwd, in_w, out_w, roots, ratio = call(
        conv_kernel,
        [big, big, spread, spread, state, state],
        [residues.T, skip.reshape(1, width), gated, grad, dec_t, pre, post],
        [state, VMEM((1, width), F32)] + [spread] * 2 + [pltpu.SemaphoreType.DMA((2,))],
        flops=8 * rows * width * modes,
        name="conv",
        hbm=2,
    )
    s = r = jnp.zeros((modes, width), F32)
    for stride in (1, 4):
        parts = [z] + [exchange(z, k * stride, size) for k in (2, 3, 1)]
        z, s, r = call(
            functools.partial(combine_kernel, stride, rows),
            [block, state, state],
            [*parts, dec_t, s, r] + [roots] * (stride == 1),
            name=f"combine{stride}",
        )
    near = exchange(z, 48, size)
    pair = exchange(z, 16, size)
    far = exchange(near, 16, size)
    fwd, bwd, s_known, r_known, w, dq, dk, dv = call(
        functools.partial(known_kernel, 16, rows),
        [big, big, state, state, state] + [local] * 3,
        [pair, dec_t, s, r, in_w, out_w, fwd, bwd, keys, values, upstream],
        flops=4 * rows * width * modes,
        name="known",
    )
    outs = [jax.ShapeDtypeStruct((rows, width), BF16)] * 3
    outs += [jax.ShapeDtypeStruct((modes, width), F32)] * 2
    outs += [jax.ShapeDtypeStruct((1, width), F32)]
    dq, dk, dv, dres, ddec, dskip = call(
        functools.partial(finish_kernel, 16, rows),
        outs,
        [z, pair, far, near, dec_t, s, r, s_known, r_known, roots, ratio, in_w, out_w, w, fwd, bwd, keys, values, upstream, dq, dk, dv],
        [local] * 3 + [state] * 2 + [VMEM((1, width), F32), big, state, pltpu.SemaphoreType.DMA((7,))],
        name="finish",
        out_space=pltpu.HBM,
    )
    return dq, dk, dv, dres.T, ddec.T, dskip.reshape(width)


def solution(mesh):
    tokens = P("seq", "chan")
    return jax.shard_map(
        shards,
        mesh=mesh,
        in_specs=(tokens, tokens, tokens, tokens, P("chan", None), P("chan", None), P("chan")),
        out_specs=(tokens, tokens, tokens, P("chan", None), P("chan", None), P("chan")),
        check_vma=False,
    )
```

```python
import functools

import jax
import jax.numpy as jnp
from jax import lax
from jax.experimental import pallas as pl
from jax.experimental.pallas import tpu as pltpu
from jax.sharding import PartitionSpec as P

F32 = jnp.float32
BF16 = jnp.bfloat16
VMEM = pltpu.VMEM
SEGS = 8
LANES = 128
GROUP = 4
STEP = 8
PAIR = 2


def product(a, b):
    return (a.astype(F32) * b.astype(F32)).astype(BF16).astype(F32)


def lanes_of(i):
    return pl.ds(pl.multiple_of(i * LANES, LANES), LANES)


def rows_of(i, n):
    return pl.ds(pl.multiple_of(i * n, n), n)


def fetch(sems, *pairs, first=0):
    copies = [pltpu.make_async_copy(a, b, sems.at[first + i]) for i, (a, b) in enumerate(pairs)]
    for copy in copies:
        copy.start()
    return copies


def summary_kernel(
    dec_hbm, k_hbm, v_hbm, u_hbm, q_hbm,
    z_ref, gated_ref, grad_ref, pre_ref, post_ref, dec_t_ref, k_ref, v_ref, u_ref, q_ref,
    w_ref, e_ref, e1_ref, g_ref, g1_ref, p_ref, t_ref, sems,
):
    rows, width = q_ref.shape
    modes = dec_t_ref.shape[0]
    steps = rows // SEGS
    tiles = width // LANES
    columns = [pl.ds(i * LANES, LANES) for i in range(tiles)]
    pairs = [(dec_hbm, dec_t_ref)]
    for ln in columns:
        pairs += [(a.at[:, ln], b.at[:, ln]) for a, b in ((k_hbm, k_ref), (v_hbm, v_ref), (u_hbm, u_ref), (q_hbm, q_ref))]
    copies = fetch(sems, *pairs)
    copies[0].wait()
    dec_t = dec_t_ref[...]
    w_all = jnp.exp(-dec_t)
    for i in range(tiles):
        for m in range(modes):
            row = w_all[m : m + 1, i * LANES : (i + 1) * LANES]
            w_ref[i, pl.ds(m * SEGS, SEGS), :] = jnp.broadcast_to(row, (SEGS, LANES))

    blocks = range(0, steps, STEP)

    def lag_sums(i):
        lags = [None] * STEP
        for first in blocks:
            x = [gated_ref[i, pl.ds((first + j) * SEGS, SEGS), :] for j in range(STEP)]
            y = [grad_ref[i, pl.ds((first + j) * SEGS, SEGS), :] for j in range(STEP)]
            for j in range(STEP):
                for back in range(j + 1):
                    term = y[j] * x[j - back]
                    lags[back] = term if lags[back] is None else lags[back] + term
        return lags

    def weighted(low, w):
        part = w[STEP - 2] * low[STEP - 1]
        slope = part
        for j in range(STEP - 2, 0, -1):
            part = part + w[j - 1] * low[j]
            slope = slope + part
        return part + low[0], slope

    def one(base, i, lags):
        at = [pl.ds((base * PAIR + m) * SEGS, SEGS) for m in range(PAIR)]
        w = [[w_ref[i, a, :]] for a in at]
        for powers in w:
            for j in range(1, STEP):
                powers.append(powers[0] * powers[j - 1])
        zero = jnp.zeros((SEGS, LANES), F32)
        h, h1, p, t, g, g1, below, power = ([zero] * PAIR for _ in range(8))
        for first in blocks:
            x = [gated_ref[i, pl.ds((first + j) * SEGS, SEGS), :] for j in range(STEP)]
            y = [grad_ref[i, pl.ds((first + j) * SEGS, SEGS), :] for j in range(STEP)]
            for m in range(PAIR):
                into, into1 = weighted(x[::-1], w[m])
                out, out1 = weighted(y, w[m])
                if first == 0:
                    h[m], h1[m], g[m], g1[m], power[m] = into, into1, out, out1, w[m][-1]
                    continue
                p[m] = p[m] + h[m] * out
                t[m] = t[m] + (h1[m] * out + h[m] * out1)
                wh = w[m][-1] * h[m]
                h1[m] = (w[m][-1] * h1[m] + float(STEP) * wh) + into1
                h[m] = wh + into
                below[m] = below[m] + g[m]
                g[m] = g[m] + power[m] * out
                g1[m] = g1[m] + power[m] * out1
                if first + STEP < steps:
                    power[m] = power[m] * w[m][-1]
        for m in range(PAIR):
            inside, inside1 = weighted(lags, w[m])
            e_ref[i, at[m], :] = w[m][0] * h[m]
            e1_ref[i, at[m], :] = w[m][0] * (h1[m] + h[m])
            g_ref[i, at[m], :] = g[m]
            g1_ref[i, at[m], :] = g1[m] + float(STEP) * (float(len(blocks) - 1) * g[m] - below[m])
            p_ref[i, at[m], :] = w[m][0] * p[m] + inside
            t_ref[i, at[m], :] = w[m][0] * (t[m] + p[m]) + inside1

    for i, ln in enumerate(columns):
        for copy in copies[1 + 4 * i : 5 + 4 * i]:
            copy.wait()
        for seg in range(SEGS):
            for part in range(steps // 16):
                at = pl.ds(seg * steps + part * 16, 16)
                to = pl.ds(part * 16 * SEGS + seg, 16, stride=SEGS)
                gated_ref[i, to, :] = product(k_ref[at, ln], v_ref[at, ln])
                grad_ref[i, to, :] = product(u_ref[at, ln], q_ref[at, ln])
        lags = lag_sums(i)
        skip = jnp.sum(lags[0], axis=0, keepdims=True)
        z_ref[6 * modes :, ln] = jnp.broadcast_to(skip, (8, LANES)).astype(BF16)
        for base in range(modes // PAIR):
            one(base, i, lags)

    for i in range(tiles):
        ln = slice(i * LANES, (i + 1) * LANES)
        dec = dec_t[:, ln]
        w_seg = jnp.exp(dec * (-float(steps)))
        zero = jnp.zeros((modes, LANES), F32)
        s, s1, p, t = zero, zero, zero, zero
        for seg in range(SEGS):
            at = pl.ds(seg, modes, stride=SEGS)
            g, g1 = g_ref[i, at, :], g1_ref[i, at, :]
            pre_ref[i, at, :] = s
            p = p + p_ref[i, at, :] + s * g
            t = t + t_ref[i, at, :] + s1 * g + s * g1
            s1 = w_seg * (s1 + float(steps) * s) + e1_ref[i, at, :]
            s = w_seg * s + e_ref[i, at, :]
        r, r1 = zero, zero
        for seg in range(SEGS - 1, -1, -1):
            at = pl.ds(seg, modes, stride=SEGS)
            post_ref[i, at, :] = r
            r1 = w_seg * (r1 + float(steps) * r) + g1_ref[i, at, :]
            r = w_seg * r + g_ref[i, at, :]
        parts = (s, 0.25 * s - dec * s1, r, 0.25 * r - dec * r1, p, 0.5 * p - dec * t)
        for n, part in enumerate(parts):
            z_ref[n * modes : (n + 1) * modes, ln] = part.astype(BF16)


def place(stride, radix):
    at = lax.axis_index("seq")
    return lax.rem(lax.div(at, stride), radix), lax.rem(at, stride)


def conv_kernel(
    res_hbm, skip_hbm, gated_ref, grad_ref, dec_t_ref, pre_ref, post_ref,
    fwd_ref, bwd_ref, in_ref, out_ref, roots_ref, ratio_ref,
    res_t_ref, skip_ref, w_ref, a_ref, sems,
):
    copies = fetch(sems, (res_hbm, res_t_ref), (skip_hbm, skip_ref))
    tiles, rows, _ = gated_ref.shape
    modes = dec_t_ref.shape[0]
    steps = rows // SEGS
    for copy in copies:
        copy.wait()
    dec_t = dec_t_ref[...]
    roots = jnp.sqrt(dec_t)
    scale = res_t_ref[...] * roots
    roots_ref[...] = roots
    ratio_ref[...] = res_t_ref[...] / roots
    seg_at = lax.broadcasted_iota(jnp.int32, (SEGS, LANES), 0).astype(F32) * float(steps)
    for i in range(tiles):
        ln = slice(i * LANES, (i + 1) * LANES)
        for m in range(modes):
            at = pl.ds(m * SEGS, SEGS)
            d = jnp.broadcast_to(dec_t[m : m + 1, ln], (SEGS, LANES))
            a = jnp.broadcast_to(scale[m : m + 1, ln], (SEGS, LANES))
            w_ref[i, at, :] = jnp.exp(-d)
            a_ref[i, at, :] = a
            in_ref[i, at, :] = a * jnp.exp(-d * seg_at)
            out_ref[i, at, :] = a * jnp.exp(-d * (float(rows - steps + 1) - seg_at))

    def one(i, _):
        direct = jnp.broadcast_to(skip_ref[:, lanes_of(i)], (SEGS, LANES))
        for base in range(0, modes, GROUP):
            at = [pl.ds((base + m) * SEGS, SEGS) for m in range(GROUP)]
            w = [w_ref[i, x, :] for x in at]
            a = [a_ref[i, x, :] for x in at]
            h = [pre_ref[i, x, :] for x in at]
            r = [post_ref[i, x, :] for x in at]
            for j in range(steps):
                at_f = pl.ds(j * SEGS, SEGS)
                at_b = pl.ds((steps - 1 - j) * SEGS, SEGS)
                x, y = gated_ref[i, at_f, :], grad_ref[i, at_b, :]
                f = fwd_ref[i, at_f, :] if base else direct * x
                b = bwd_ref[i, at_b, :] if base else direct * y
                for m in range(GROUP):
                    h[m] = (w[m] * h[m] if j else h[m]) + x
                    r[m] = w[m] * r[m] + y
                    f = f + a[m] * h[m]
                    b = b + a[m] * r[m]
                fwd_ref[i, at_f, :] = f
                bwd_ref[i, at_b, :] = b
        return 0

    lax.fori_loop(0, tiles, one, 0)


def rows_in(seg, part, steps):
    return pl.ds(seg * steps + part * 16, 16), pl.ds(part * 16 * SEGS + seg, 16, stride=SEGS)


def query_rows(u_ref, total_ref, dq_ref, i, frm, to, ln):
    conv = total_ref[i, frm, :].astype(BF16).astype(F32)
    dq_ref[to, ln] = (u_ref[to, ln].astype(F32) * conv).astype(BF16)


def pair_rows(k_ref, v_ref, total_ref, dk_ref, dv_ref, i, frm, to, ln):
    gg = total_ref[i, frm, :].astype(BF16).astype(F32)
    dk_ref[to, ln] = (gg * v_ref[to, ln].astype(F32)).astype(BF16)
    dv_ref[to, ln] = (gg * k_ref[to, ln].astype(F32)).astype(BF16)


def add_state(local_ref, total_ref, scale_ref, state_ref, w_ref, order, tiles, modes):
    def one(i, _):
        ln = lanes_of(i)

        def spread(ref, m):
            return jnp.broadcast_to(ref[pl.ds(m, 1), ln], (SEGS, LANES))

        w = [spread(w_ref, m) for m in range(modes)]
        c = [scale_ref[i, pl.ds(m * SEGS, SEGS), :] * spread(state_ref, m) for m in range(modes)]
        for n, j in enumerate(order):
            here = pl.ds(j * SEGS, SEGS)
            y = local_ref[i, here, :]
            for m in range(modes):
                y = y + c[m]
                if n < len(order) - 1:
                    c[m] = c[m] * w[m]
            total_ref[i, here, :] = y
        return 0

    lax.fori_loop(0, tiles, one, 0)


def known_kernel(
    stride, count,
    pair_ref, dec_t_ref, s_ref, r_ref, in_ref, out_ref, fwd_old, bwd_old, k_ref, v_ref, u_ref,
    fwd_ref, bwd_ref, s_out, r_out, w_ref, dq_ref, dk_ref, dv_ref,
):
    tiles, rows, _ = fwd_ref.shape
    modes = dec_t_ref.shape[0]
    steps = rows // SEGS
    digit, offset = place(stride, 2)
    offset = offset.astype(F32)
    dec_t = dec_t_ref[...]
    enter = jnp.exp(dec_t * (-float(count) * offset)) * pair_ref[pl.ds(0, modes), :].astype(F32)
    leave = jnp.exp(dec_t * (-float(count) * (float(stride - 1) - offset))) * pair_ref[pl.ds(2 * modes, modes), :].astype(F32)
    s_out[...] = s_ref[...] + jnp.where(digit == 1, enter, 0.0)
    r_out[...] = r_ref[...] + jnp.where(digit == 1, 0.0, leave)
    w_ref[...] = jnp.exp(-dec_t)
    add_state(fwd_old, fwd_ref, in_ref, s_out, w_ref, range(steps), tiles, modes)
    add_state(bwd_old, bwd_ref, out_ref, r_out, w_ref, range(steps - 1, -1, -1), tiles, modes)
    for seg in range(SEGS):
        for part in range(steps // 16):
            to, frm = rows_in(seg, part, steps)
            for i in range(tiles):
                ln = pl.ds(i * LANES, LANES)
                query_rows(u_ref, fwd_ref, dq_ref, i, frm, to, ln)
                pair_rows(k_ref, v_ref, bwd_ref, dk_ref, dv_ref, i, frm, to, ln)


def combine(stride, count, parts, dec_t, s, r):
    modes = dec_t.shape[0]
    digit, offset = place(stride, 4)
    offset = offset.astype(F32)
    odd, high = lax.rem(digit, 2) == 1, digit >= 2

    def gather(i, n=modes):
        a, b, c, d = (parts(k, i, n) for k in range(4))
        a, b = lax.select(odd, b, a), lax.select(odd, a, b)
        c, d = lax.select(odd, d, c), lax.select(odd, c, d)
        a, c = lax.select(high, c, a), lax.select(high, a, c)
        b, d = lax.select(high, d, b), lax.select(high, b, d)
        return [x.astype(F32) for x in (a, b, c, d)]

    e, f, g, h, p, d = (gather(i) for i in range(6))
    k = gather(6, 8)
    one = dec_t * float(count * stride)
    w = [None, jnp.exp(-one)]
    w += [w[1] * w[1], w[1] * w[1] * w[1]]
    e_t, f_t, g_t, h_t, p_t, d_t, k_t = e[0], f[0], g[0], h[0], p[0], d[0], k[0]
    enter = jnp.zeros_like(dec_t)
    for j in range(1, 4):
        enter = jnp.where(digit == j, e_t, enter)
        p_t = p_t + p[j] + e_t * g[j]
        d_t = d_t + d[j] + f_t * g[j] + e_t * h[j]
        f_t = w[1] * (f_t - one * e_t) + f[j]
        e_t = w[1] * e_t + e[j]
        h_t = h_t + w[j] * (h[j] - one * float(j) * g[j])
        g_t = g_t + w[j] * g[j]
        k_t = k_t + k[j]
    leave = jnp.zeros_like(dec_t)
    tail = g[3]
    for j in range(2, -1, -1):
        leave = jnp.where(digit == j, tail, leave)
        tail = g[j] + w[1] * tail
    s = s + jnp.exp(dec_t * (-float(count) * offset)) * enter
    r = r + jnp.exp(dec_t * (-float(count) * (float(stride - 1) - offset))) * leave
    return (e_t, f_t, g_t, h_t, p_t, d_t, k_t), s, r


def combine_kernel(stride, count, z0, z2, z3, z1, dec_t_ref, s_ref, r_ref, *refs):
    z_ref, s_out, r_out = refs[-3:]
    modes = dec_t_ref.shape[0]

    def parts(k, i, n):
        return (z0, z1, z2, z3)[k][pl.ds(i * modes, n), :]

    block, s_out[...], r_out[...] = combine(stride, count, parts, dec_t_ref[...], s_ref[...], r_ref[...])
    for i, part in enumerate(block):
        z_ref[pl.ds(i * modes, part.shape[0]), :] = part.astype(BF16)


def finish_kernel(
    stride, count,
    own_ref, pair_ref, far_ref, near_ref, dec_t_ref, s_ref, r_ref, s_known, r_known,
    roots_ref, ratio_ref, in_ref, out_ref, w_ref, fwd_ref, bwd_ref,
    k_ref, v_ref, u_ref, dq_old, dk_old, dv_old,
    dq_hbm, dk_hbm, dv_hbm, dres_hbm, ddec_hbm, dskip_hbm,
    dq_ref, dk_ref, dv_ref, dres_ref, ddec_ref, dskip_ref, total_ref, c_ref, sems,
):
    rows, width = k_ref.shape
    modes = w_ref.shape[0]
    steps = rows // SEGS
    tiles = width // LANES
    right = place(2 * stride, 2)[0] == 1
    outs = ((dq_old, dq_ref, dq_hbm), (dk_old, dk_ref, dk_hbm), (dv_old, dv_ref, dv_hbm))

    @pl.when(right)
    def _():
        fetch(sems, *[(old, hbm) for old, _, hbm in outs[1:]])

    @pl.when(jnp.logical_not(right))
    def _():
        fetch(sems, *[(old, hbm) for old, _, hbm in outs[:1]])

    def parts(k, i, n):
        return (own_ref, pair_ref, far_ref, near_ref)[k][pl.ds(i * modes, n), :]

    block, s, r = combine(stride, count, parts, dec_t_ref[...], s_ref[...], r_ref[...])
    c_ref[...] = jnp.where(right, s - s_known[...], r - r_known[...])
    dres_ref[...] = roots_ref[...] * block[4]
    ddec_ref[...] = ratio_ref[...] * block[5]
    dskip_ref[...] = block[6][:1]
    copies = fetch(sems, (dres_ref, dres_hbm), (ddec_ref, ddec_hbm), (dskip_ref, dskip_hbm), first=2)

    def rest(work, pairs):
        for seg in range(SEGS):
            for part in range(steps // 16):
                to, frm = rows_in(seg, part, steps)
                for i in range(tiles):
                    work(i, frm, to, pl.ds(i * LANES, LANES))
        done = fetch(sems, *pairs, first=5)
        for copy in done:
            copy.wait()

    @pl.when(right)
    def _():
        add_state(fwd_ref, total_ref, in_ref, c_ref, w_ref, range(steps), tiles, modes)
        rest(
            lambda i, frm, to, ln: query_rows(u_ref, total_ref, dq_ref, i, frm, to, ln),
            [(new, hbm) for _, new, hbm in outs[:1]],
        )
        for i, (old, _, hbm) in enumerate(outs[1:]):
            pltpu.make_async_copy(old, hbm, sems.at[i]).wait()

    @pl.when(jnp.logical_not(right))
    def _():
        add_state(bwd_ref, total_ref, out_ref, c_ref, w_ref, range(steps - 1, -1, -1), tiles, modes)
        rest(
            lambda i, frm, to, ln: pair_rows(k_ref, v_ref, total_ref, dk_ref, dv_ref, i, frm, to, ln),
            [(new, hbm) for _, new, hbm in outs[1:]],
        )
        pltpu.make_async_copy(dq_old, dq_hbm, sems.at[0]).wait()

    for copy in copies:
        copy.wait()


def kept(array, space=VMEM):
    return pltpu.with_memory_space_constraint(array, space)


def call(kernel, outs, args, scratch=(), flops=0, name=None, hbm=0, out_space=VMEM):
    return pl.pallas_call(
        kernel,
        out_shape=outs,
        in_specs=[pl.BlockSpec(memory_space=pltpu.HBM)] * hbm + [pl.BlockSpec(memory_space=VMEM)] * (len(args) - hbm),
        out_specs=[pl.BlockSpec(memory_space=out_space)] * len(outs),
        scratch_shapes=list(scratch),
        cost_estimate=pl.CostEstimate(flops=flops, bytes_accessed=1 << 19, transcendentals=0),
        compiler_params=pltpu.CompilerParams(vmem_limit_bytes=24 << 20),
        name=name,
    )(*[kept(a, pltpu.HBM) for a in args[:hbm]], *[kept(a) for a in args[hbm:]])


def exchange(array, mask, size):
    return lax.ppermute(array, "seq", [(i, i ^ mask) for i in range(size)])


def shards(queries, keys, values, upstream, residues, decay, skip):
    rows, width = queries.shape
    modes = residues.shape[1]
    size = lax.axis_size("seq")
    seg_rows = modes * SEGS
    z_rows = 6 * modes + 8
    tiles = width // LANES
    big = VMEM((tiles, rows, LANES), F32)
    state = VMEM((modes, width), F32)
    spread = VMEM((tiles, seg_rows, LANES), F32)
    block = VMEM((z_rows, width), BF16)
    local = VMEM((rows, width), BF16)
    z, gated, grad, pre, post, dec_t, keys, values, upstream, queries = call(
        summary_kernel,
        [block, big, big, spread, spread, state] + [local] * 4,
        [decay.T, keys, values, upstream, queries],
        [spread] * 7 + [pltpu.SemaphoreType.DMA((1 + 4 * tiles,))],
        flops=12 * rows * width * modes,
        name="summary",
        hbm=5,
    )
    fwd, bwd, in_w, out_w, roots, ratio = call(
        conv_kernel,
        [big, big, spread, spread, state, state],
        [residues.T, skip.reshape(1, width), gated, grad, dec_t, pre, post],
        [state, VMEM((1, width), F32)] + [spread] * 2 + [pltpu.SemaphoreType.DMA((2,))],
        flops=8 * rows * width * modes,
        name="conv",
        hbm=2,
    )
    s = r = jnp.zeros((modes, width), F32)
    for stride in (1, 4):
        parts = [z] + [exchange(z, k * stride, size) for k in (2, 3, 1)]
        z, s, r = call(
            functools.partial(combine_kernel, stride, rows),
            [block, state, state],
            [*parts, dec_t, s, r] + [roots] * (stride == 1),
            name=f"combine{stride}",
        )
    near = exchange(z, 48, size)
    pair = exchange(z, 16, size)
    far = exchange(near, 16, size)
    fwd, bwd, s_known, r_known, w, dq, dk, dv = call(
        functools.partial(known_kernel, 16, rows),
        [big, big, state, state, state] + [local] * 3,
        [pair, dec_t, s, r, in_w, out_w, fwd, bwd, keys, values, upstream],
        flops=4 * rows * width * modes,
        name="known",
    )
    outs = [jax.ShapeDtypeStruct((rows, width), BF16)] * 3
    outs += [jax.ShapeDtypeStruct((modes, width), F32)] * 2
    outs += [jax.ShapeDtypeStruct((1, width), F32)]
    dq, dk, dv, dres, ddec, dskip = call(
        functools.partial(finish_kernel, 16, rows),
        outs,
        [z, pair, far, near, dec_t, s, r, s_known, r_known, roots, ratio, in_w, out_w, w, fwd, bwd, keys, values, upstream, dq, dk, dv],
        [local] * 3 + [state] * 2 + [VMEM((1, width), F32), big, state, pltpu.SemaphoreType.DMA((7,))],
        name="finish",
        out_space=pltpu.HBM,
    )
    return dq, dk, dv, dres.T, ddec.T, dskip.reshape(width)


def solution(mesh):
    tokens = P("seq", "chan")
    return jax.shard_map(
        shards,
        mesh=mesh,
        in_specs=(tokens, tokens, tokens, tokens, P("chan", None), P("chan", None), P("chan")),
        out_specs=(tokens, tokens, tokens, P("chan", None), P("chan", None), P("chan")),
        check_vma=False,
    )
```

```python
import functools

import jax
import jax.numpy as jnp
from jax import lax
from jax.experimental import pallas as pl
from jax.experimental.pallas import tpu as pltpu
from jax.sharding import PartitionSpec as P

F32 = jnp.float32
BF16 = jnp.bfloat16
VMEM = pltpu.VMEM
SEGS = 8
LANES = 128
GROUP = 4
STEP = 8
PAIR = 2


def product(a, b):
    return (a.astype(F32) * b.astype(F32)).astype(BF16).astype(F32)


def lanes_of(i):
    return pl.ds(pl.multiple_of(i * LANES, LANES), LANES)


def rows_of(i, n):
    return pl.ds(pl.multiple_of(i * n, n), n)


def fetch(sems, *pairs, first=0):
    copies = [pltpu.make_async_copy(a, b, sems.at[first + i]) for i, (a, b) in enumerate(pairs)]
    for copy in copies:
        copy.start()
    return copies


def summary_kernel(
    dec_hbm, k_hbm, v_hbm, u_hbm, q_hbm,
    z_ref, gated_ref, grad_ref, pre_ref, post_ref, dec_t_ref, k_ref, v_ref, u_ref, q_ref,
    w_ref, e_ref, e1_ref, g_ref, g1_ref, p_ref, t_ref, sems,
):
    rows, width = q_ref.shape
    modes = dec_t_ref.shape[0]
    steps = rows // SEGS
    tiles = width // LANES
    columns = [pl.ds(i * LANES, LANES) for i in range(tiles)]
    pairs = [(dec_hbm, dec_t_ref)]
    for ln in columns:
        pairs += [(a.at[:, ln], b.at[:, ln]) for a, b in ((k_hbm, k_ref), (v_hbm, v_ref), (u_hbm, u_ref), (q_hbm, q_ref))]
    copies = fetch(sems, *pairs)
    copies[0].wait()
    dec_t = dec_t_ref[...]
    w_all = jnp.exp(-dec_t)
    for i in range(tiles):
        for m in range(modes):
            row = w_all[m : m + 1, i * LANES : (i + 1) * LANES]
            w_ref[i, pl.ds(m * SEGS, SEGS), :] = jnp.broadcast_to(row, (SEGS, LANES))

    blocks = range(0, steps, STEP)

    def lag_sums(i):
        lags = [None] * STEP
        for first in blocks:
            x = [gated_ref[i, pl.ds((first + j) * SEGS, SEGS), :] for j in range(STEP)]
            y = [grad_ref[i, pl.ds((first + j) * SEGS, SEGS), :] for j in range(STEP)]
            for j in range(STEP):
                for back in range(j + 1):
                    term = y[j] * x[j - back]
                    lags[back] = term if lags[back] is None else lags[back] + term
        return lags

    def weighted(low, w):
        part = w[STEP - 2] * low[STEP - 1]
        slope = part
        for j in range(STEP - 2, 0, -1):
            part = part + w[j - 1] * low[j]
            slope = slope + part
        return part + low[0], slope

    def one(base, i, lags):
        at = [pl.ds((base * PAIR + m) * SEGS, SEGS) for m in range(PAIR)]
        w = [[w_ref[i, a, :]] for a in at]
        for powers in w:
            for j in range(1, STEP):
                powers.append(powers[0] * powers[j - 1])
        zero = jnp.zeros((SEGS, LANES), F32)
        h, h1, p, t, g, g1, below, power = ([zero] * PAIR for _ in range(8))
        for first in blocks:
            x = [gated_ref[i, pl.ds((first + j) * SEGS, SEGS), :] for j in range(STEP)]
            y = [grad_ref[i, pl.ds((first + j) * SEGS, SEGS), :] for j in range(STEP)]
            for m in range(PAIR):
                into, into1 = weighted(x[::-1], w[m])
                out, out1 = weighted(y, w[m])
                if first == 0:
                    h[m], h1[m], g[m], g1[m], power[m] = into, into1, out, out1, w[m][-1]
                    continue
                p[m] = p[m] + h[m] * out
                t[m] = t[m] + (h1[m] * out + h[m] * out1)
                wh = w[m][-1] * h[m]
                h1[m] = (w[m][-1] * h1[m] + float(STEP) * wh) + into1
                h[m] = wh + into
                below[m] = below[m] + g[m]
                g[m] = g[m] + power[m] * out
                g1[m] = g1[m] + power[m] * out1
                if first + STEP < steps:
                    power[m] = power[m] * w[m][-1]
        for m in range(PAIR):
            inside, inside1 = weighted(lags, w[m])
            e_ref[i, at[m], :] = w[m][0] * h[m]
            e1_ref[i, at[m], :] = w[m][0] * (h1[m] + h[m])
            g_ref[i, at[m], :] = g[m]
            g1_ref[i, at[m], :] = g1[m] + float(STEP) * (float(len(blocks) - 1) * g[m] - below[m])
            p_ref[i, at[m], :] = w[m][0] * p[m] + inside
            t_ref[i, at[m], :] = w[m][0] * (t[m] + p[m]) + inside1

    for i, ln in enumerate(columns):
        for copy in copies[1 + 4 * i : 5 + 4 * i]:
            copy.wait()
        for seg in range(SEGS):
            for part in range(steps // 16):
                at = pl.ds(seg * steps + part * 16, 16)
                to = pl.ds(part * 16 * SEGS + seg, 16, stride=SEGS)
                gated_ref[i, to, :] = product(k_ref[at, ln], v_ref[at, ln])
                grad_ref[i, to, :] = product(u_ref[at, ln], q_ref[at, ln])
        lags = lag_sums(i)
        skip = jnp.sum(lags[0], axis=0, keepdims=True)
        z_ref[6 * modes :, ln] = jnp.broadcast_to(skip, (8, LANES)).astype(BF16)
        for base in range(modes // PAIR):
            one(base, i, lags)

    for i in range(tiles):
        ln = slice(i * LANES, (i + 1) * LANES)
        dec = dec_t[:, ln]
        w_seg = jnp.exp(dec * (-float(steps)))
        zero = jnp.zeros((modes, LANES), F32)
        s, s1, p, t = zero, zero, zero, zero
        for seg in range(SEGS):
            at = pl.ds(seg, modes, stride=SEGS)
            g, g1 = g_ref[i, at, :], g1_ref[i, at, :]
            pre_ref[i, at, :] = s
            p = p + p_ref[i, at, :] + s * g
            t = t + t_ref[i, at, :] + s1 * g + s * g1
            s1 = w_seg * (s1 + float(steps) * s) + e1_ref[i, at, :]
            s = w_seg * s + e_ref[i, at, :]
        r, r1 = zero, zero
        for seg in range(SEGS - 1, -1, -1):
            at = pl.ds(seg, modes, stride=SEGS)
            post_ref[i, at, :] = r
            r1 = w_seg * (r1 + float(steps) * r) + g1_ref[i, at, :]
            r = w_seg * r + g_ref[i, at, :]
        parts = (s, 0.25 * s - dec * s1, r, 0.25 * r - dec * r1, p, 0.5 * p - dec * t)
        for n, part in enumerate(parts):
            z_ref[n * modes : (n + 1) * modes, ln] = part.astype(BF16)


def place(stride, radix):
    at = lax.axis_index("seq")
    return lax.rem(lax.div(at, stride), radix), lax.rem(at, stride)


def conv_kernel(
    res_hbm, skip_hbm, gated_ref, grad_ref, dec_t_ref, pre_ref, post_ref,
    fwd_ref, bwd_ref, in_ref, out_ref, roots_ref, ratio_ref,
    res_t_ref, skip_ref, w_ref, a_ref, sems,
):
    copies = fetch(sems, (res_hbm, res_t_ref), (skip_hbm, skip_ref))
    tiles, rows, _ = gated_ref.shape
    modes = dec_t_ref.shape[0]
    steps = rows // SEGS
    for copy in copies:
        copy.wait()
    dec_t = dec_t_ref[...]
    roots = jnp.sqrt(dec_t)
    scale = res_t_ref[...] * roots
    roots_ref[...] = roots
    ratio_ref[...] = res_t_ref[...] / roots
    seg_at = lax.broadcasted_iota(jnp.int32, (SEGS, LANES), 0).astype(F32) * float(steps)
    for i in range(tiles):
        ln = slice(i * LANES, (i + 1) * LANES)
        for m in range(modes):
            at = pl.ds(m * SEGS, SEGS)
            d = jnp.broadcast_to(dec_t[m : m + 1, ln], (SEGS, LANES))
            a = jnp.broadcast_to(scale[m : m + 1, ln], (SEGS, LANES))
            w_ref[i, at, :] = jnp.exp(-d)
            a_ref[i, at, :] = a
            in_ref[i, at, :] = a * jnp.exp(-d * seg_at)
            out_ref[i, at, :] = a * jnp.exp(-d * (float(rows - steps + 1) - seg_at))

    def one(i, _):
        direct = jnp.broadcast_to(skip_ref[:, lanes_of(i)], (SEGS, LANES))
        for base in range(0, modes, GROUP):
            at = [pl.ds((base + m) * SEGS, SEGS) for m in range(GROUP)]
            w = [w_ref[i, x, :] for x in at]
            a = [a_ref[i, x, :] for x in at]
            h = [pre_ref[i, x, :] for x in at]
            r = [post_ref[i, x, :] for x in at]
            for j in range(steps):
                at_f = pl.ds(j * SEGS, SEGS)
                at_b = pl.ds((steps - 1 - j) * SEGS, SEGS)
                x, y = gated_ref[i, at_f, :], grad_ref[i, at_b, :]
                f = fwd_ref[i, at_f, :] if base else direct * x
                b = bwd_ref[i, at_b, :] if base else direct * y
                for m in range(GROUP):
                    h[m] = (w[m] * h[m] if j else h[m]) + x
                    r[m] = w[m] * r[m] + y
                    f = f + a[m] * h[m]
                    b = b + a[m] * r[m]
                fwd_ref[i, at_f, :] = f
                bwd_ref[i, at_b, :] = b
        return 0

    lax.fori_loop(0, tiles, one, 0)


def rows_in(seg, part, steps):
    return pl.ds(seg * steps + part * 16, 16), pl.ds(part * 16 * SEGS + seg, 16, stride=SEGS)


def query_rows(u_ref, total_ref, dq_ref, i, frm, to, ln):
    conv = total_ref[i, frm, :].astype(BF16).astype(F32)
    dq_ref[to, ln] = (u_ref[to, ln].astype(F32) * conv).astype(BF16)


def pair_rows(k_ref, v_ref, total_ref, dk_ref, dv_ref, i, frm, to, ln):
    gg = total_ref[i, frm, :].astype(BF16).astype(F32)
    dk_ref[to, ln] = (gg * v_ref[to, ln].astype(F32)).astype(BF16)
    dv_ref[to, ln] = (gg * k_ref[to, ln].astype(F32)).astype(BF16)


def add_state(local_ref, total_ref, scale_ref, state_ref, w_ref, order, tiles, modes):
    def one(i):
        ln = pl.ds(i * LANES, LANES)

        def spread(ref, m):
            return jnp.broadcast_to(ref[pl.ds(m, 1), ln], (SEGS, LANES))

        w = [spread(w_ref, m) for m in range(modes)]
        c = [scale_ref[i, pl.ds(m * SEGS, SEGS), :] * spread(state_ref, m) for m in range(modes)]
        for n, j in enumerate(order):
            here = pl.ds(j * SEGS, SEGS)
            y = local_ref[i, here, :]
            for m in range(modes):
                y = y + c[m]
                if n < len(order) - 1:
                    c[m] = c[m] * w[m]
            total_ref[i, here, :] = y

    for i in range(tiles):
        one(i)


def known_kernel(
    stride, count,
    pair_ref, dec_t_ref, s_ref, r_ref, in_ref, out_ref, fwd_old, bwd_old, k_ref, v_ref, u_ref,
    fwd_ref, bwd_ref, s_out, r_out, w_ref, dq_ref, dk_ref, dv_ref,
):
    tiles, rows, _ = fwd_ref.shape
    modes = dec_t_ref.shape[0]
    steps = rows // SEGS
    digit, offset = place(stride, 2)
    offset = offset.astype(F32)
    dec_t = dec_t_ref[...]
    enter = jnp.exp(dec_t * (-float(count) * offset)) * pair_ref[pl.ds(0, modes), :].astype(F32)
    leave = jnp.exp(dec_t * (-float(count) * (float(stride - 1) - offset))) * pair_ref[pl.ds(2 * modes, modes), :].astype(F32)
    s_out[...] = s_ref[...] + jnp.where(digit == 1, enter, 0.0)
    r_out[...] = r_ref[...] + jnp.where(digit == 1, 0.0, leave)
    w_ref[...] = jnp.exp(-dec_t)
    add_state(fwd_old, fwd_ref, in_ref, s_out, w_ref, range(steps), tiles, modes)
    add_state(bwd_old, bwd_ref, out_ref, r_out, w_ref, range(steps - 1, -1, -1), tiles, modes)
    for seg in range(SEGS):
        for part in range(steps // 16):
            to, frm = rows_in(seg, part, steps)
            for i in range(tiles):
                ln = pl.ds(i * LANES, LANES)
                query_rows(u_ref, fwd_ref, dq_ref, i, frm, to, ln)
                pair_rows(k_ref, v_ref, bwd_ref, dk_ref, dv_ref, i, frm, to, ln)


def combine(stride, count, parts, dec_t, s, r):
    modes = dec_t.shape[0]
    digit, offset = place(stride, 4)
    offset = offset.astype(F32)
    odd, high = lax.rem(digit, 2) == 1, digit >= 2

    def gather(i, n=modes):
        a, b, c, d = (parts(k, i, n) for k in range(4))
        a, b = lax.select(odd, b, a), lax.select(odd, a, b)
        c, d = lax.select(odd, d, c), lax.select(odd, c, d)
        a, c = lax.select(high, c, a), lax.select(high, a, c)
        b, d = lax.select(high, d, b), lax.select(high, b, d)
        return [x.astype(F32) for x in (a, b, c, d)]

    e, f, g, h, p, d = (gather(i) for i in range(6))
    k = gather(6, 8)
    one = dec_t * float(count * stride)
    w = [None, jnp.exp(-one)]
    w += [w[1] * w[1], w[1] * w[1] * w[1]]
    e_t, f_t, g_t, h_t, p_t, d_t, k_t = e[0], f[0], g[0], h[0], p[0], d[0], k[0]
    enter = jnp.zeros_like(dec_t)
    for j in range(1, 4):
        enter = jnp.where(digit == j, e_t, enter)
        p_t = p_t + p[j] + e_t * g[j]
        d_t = d_t + d[j] + f_t * g[j] + e_t * h[j]
        f_t = w[1] * (f_t - one * e_t) + f[j]
        e_t = w[1] * e_t + e[j]
        h_t = h_t + w[j] * (h[j] - one * float(j) * g[j])
        g_t = g_t + w[j] * g[j]
        k_t = k_t + k[j]
    leave = jnp.zeros_like(dec_t)
    tail = g[3]
    for j in range(2, -1, -1):
        leave = jnp.where(digit == j, tail, leave)
        tail = g[j] + w[1] * tail
    s = s + jnp.exp(dec_t * (-float(count) * offset)) * enter
    r = r + jnp.exp(dec_t * (-float(count) * (float(stride - 1) - offset))) * leave
    return (e_t, f_t, g_t, h_t, p_t, d_t, k_t), s, r


def combine_kernel(stride, count, z0, z2, z3, z1, dec_t_ref, s_ref, r_ref, *refs):
    z_ref, s_out, r_out = refs[-3:]
    modes = dec_t_ref.shape[0]

    def parts(k, i, n):
        return (z0, z1, z2, z3)[k][pl.ds(i * modes, n), :]

    block, s_out[...], r_out[...] = combine(stride, count, parts, dec_t_ref[...], s_ref[...], r_ref[...])
    for i, part in enumerate(block):
        z_ref[pl.ds(i * modes, part.shape[0]), :] = part.astype(BF16)


def finish_kernel(
    stride, count,
    own_ref, pair_ref, far_ref, near_ref, dec_t_ref, s_ref, r_ref, s_known, r_known,
    roots_ref, ratio_ref, in_ref, out_ref, w_ref, fwd_ref, bwd_ref,
    k_ref, v_ref, u_ref, dq_old, dk_old, dv_old,
    dq_hbm, dk_hbm, dv_hbm, dres_hbm, ddec_hbm, dskip_hbm,
    dq_ref, dk_ref, dv_ref, dres_ref, ddec_ref, dskip_ref, total_ref, c_ref, sems,
):
    rows, width = k_ref.shape
    modes = w_ref.shape[0]
    steps = rows // SEGS
    tiles = width // LANES
    right = place(2 * stride, 2)[0] == 1
    outs = ((dq_old, dq_ref, dq_hbm), (dk_old, dk_ref, dk_hbm), (dv_old, dv_ref, dv_hbm))

    @pl.when(right)
    def _():
        fetch(sems, *[(old, hbm) for old, _, hbm in outs[1:]])

    @pl.when(jnp.logical_not(right))
    def _():
        fetch(sems, *[(old, hbm) for old, _, hbm in outs[:1]])

    def parts(k, i, n):
        return (own_ref, pair_ref, far_ref, near_ref)[k][pl.ds(i * modes, n), :]

    block, s, r = combine(stride, count, parts, dec_t_ref[...], s_ref[...], r_ref[...])
    c_ref[...] = jnp.where(right, s - s_known[...], r - r_known[...])
    dres_ref[...] = roots_ref[...] * block[4]
    ddec_ref[...] = ratio_ref[...] * block[5]
    dskip_ref[...] = block[6][:1]
    copies = fetch(sems, (dres_ref, dres_hbm), (ddec_ref, ddec_hbm), (dskip_ref, dskip_hbm), first=2)

    def rest(work, pairs):
        for seg in range(SEGS):
            for part in range(steps // 16):
                to, frm = rows_in(seg, part, steps)
                for i in range(tiles):
                    work(i, frm, to, pl.ds(i * LANES, LANES))
        done = fetch(sems, *pairs, first=5)
        for copy in done:
            copy.wait()

    @pl.when(right)
    def _():
        add_state(fwd_ref, total_ref, in_ref, c_ref, w_ref, range(steps), tiles, modes)
        rest(
            lambda i, frm, to, ln: query_rows(u_ref, total_ref, dq_ref, i, frm, to, ln),
            [(new, hbm) for _, new, hbm in outs[:1]],
        )
        for i, (old, _, hbm) in enumerate(outs[1:]):
            pltpu.make_async_copy(old, hbm, sems.at[i]).wait()

    @pl.when(jnp.logical_not(right))
    def _():
        add_state(bwd_ref, total_ref, out_ref, c_ref, w_ref, range(steps - 1, -1, -1), tiles, modes)
        rest(
            lambda i, frm, to, ln: pair_rows(k_ref, v_ref, total_ref, dk_ref, dv_ref, i, frm, to, ln),
            [(new, hbm) for _, new, hbm in outs[1:]],
        )
        pltpu.make_async_copy(dq_old, dq_hbm, sems.at[0]).wait()

    for copy in copies:
        copy.wait()


def kept(array, space=VMEM):
    return pltpu.with_memory_space_constraint(array, space)


def call(kernel, outs, args, scratch=(), flops=0, name=None, hbm=0, out_space=VMEM):
    return pl.pallas_call(
        kernel,
        out_shape=outs,
        in_specs=[pl.BlockSpec(memory_space=pltpu.HBM)] * hbm + [pl.BlockSpec(memory_space=VMEM)] * (len(args) - hbm),
        out_specs=[pl.BlockSpec(memory_space=out_space)] * len(outs),
        scratch_shapes=list(scratch),
        cost_estimate=pl.CostEstimate(flops=flops, bytes_accessed=1 << 19, transcendentals=0),
        compiler_params=pltpu.CompilerParams(vmem_limit_bytes=24 << 20),
        name=name,
    )(*[kept(a, pltpu.HBM) for a in args[:hbm]], *[kept(a) for a in args[hbm:]])


def exchange(array, mask, size):
    return lax.ppermute(array, "seq", [(i, i ^ mask) for i in range(size)])


def shards(queries, keys, values, upstream, residues, decay, skip):
    rows, width = queries.shape
    modes = residues.shape[1]
    size = lax.axis_size("seq")
    seg_rows = modes * SEGS
    z_rows = 6 * modes + 8
    tiles = width // LANES
    big = VMEM((tiles, rows, LANES), F32)
    state = VMEM((modes, width), F32)
    spread = VMEM((tiles, seg_rows, LANES), F32)
    block = VMEM((z_rows, width), BF16)
    local = VMEM((rows, width), BF16)
    z, gated, grad, pre, post, dec_t, keys, values, upstream, queries = call(
        summary_kernel,
        [block, big, big, spread, spread, state] + [local] * 4,
        [decay.T, keys, values, upstream, queries],
        [spread] * 7 + [pltpu.SemaphoreType.DMA((1 + 4 * tiles,))],
        flops=12 * rows * width * modes,
        name="summary",
        hbm=5,
    )
    fwd, bwd, in_w, out_w, roots, ratio = call(
        conv_kernel,
        [big, big, spread, spread, state, state],
        [residues.T, skip.reshape(1, width), gated, grad, dec_t, pre, post],
        [state, VMEM((1, width), F32)] + [spread] * 2 + [pltpu.SemaphoreType.DMA((2,))],
        flops=8 * rows * width * modes,
        name="conv",
        hbm=2,
    )
    s = r = jnp.zeros((modes, width), F32)
    for stride in (1, 4):
        parts = [z] + [exchange(z, k * stride, size) for k in (2, 3, 1)]
        z, s, r = call(
            functools.partial(combine_kernel, stride, rows),
            [block, state, state],
            [*parts, dec_t, s, r] + [roots] * (stride == 1),
            name=f"combine{stride}",
        )
    near = exchange(z, 48, size)
    pair = exchange(z, 16, size)
    far = exchange(near, 16, size)
    fwd, bwd, s_known, r_known, w, dq, dk, dv = call(
        functools.partial(known_kernel, 16, rows),
        [big, big, state, state, state] + [local] * 3,
        [pair, dec_t, s, r, in_w, out_w, fwd, bwd, keys, values, upstream],
        flops=4 * rows * width * modes,
        name="known",
    )
    outs = [jax.ShapeDtypeStruct((rows, width), BF16)] * 3
    outs += [jax.ShapeDtypeStruct((modes, width), F32)] * 2
    outs += [jax.ShapeDtypeStruct((1, width), F32)]
    dq, dk, dv, dres, ddec, dskip = call(
        functools.partial(finish_kernel, 16, rows),
        outs,
        [z, pair, far, near, dec_t, s, r, s_known, r_known, roots, ratio, in_w, out_w, w, fwd, bwd, keys, values, upstream, dq, dk, dv],
        [local] * 3 + [state] * 2 + [VMEM((1, width), F32), big, state, pltpu.SemaphoreType.DMA((7,))],
        name="finish",
        out_space=pltpu.HBM,
    )
    return dq, dk, dv, dres.T, ddec.T, dskip.reshape(width)


def solution(mesh):
    tokens = P("seq", "chan")
    return jax.shard_map(
        shards,
        mesh=mesh,
        in_specs=(tokens, tokens, tokens, tokens, P("chan", None), P("chan", None), P("chan")),
        out_specs=(tokens, tokens, tokens, P("chan", None), P("chan", None), P("chan")),
        check_vma=False,
    )
```
